256 devices in a mesh: cache: 32 (over z, x), tensor: 8 (over y, core).
Axes of the slice: x: 4, y: 4, z: 8, core: 2. Of those that a mesh axis runs over, the one named last changes fastest.
Arguments:
- queries: bfloat16 [256, 4, 8192], P('cache', None, 'tensor'), may hold values from -12 to 12
- new_kv: bfloat16 [256, 4, 2, 1024], P('cache', None, None, 'tensor'), may hold values from -12 to 12
- prefix_kv: bfloat16 [2, 196608, 1024], P(None, 'cache', 'tensor'), may hold values from -6 to 6
- suffix_kv: bfloat16 [256, 2, 512, 1024], P('cache', None, None, 'tensor'), may hold values from -9 to 9
- suffix_len: int32 [256], P('cache'), may hold values from 1 to 512, as said below
- branch_prompt: int32 [256, 1], P('cache'), may hold values from 0 to 7; in each aligned block of 8 rows (0 to 7, 8 to 15, ...) at most 2 rows name the same one
- out_weight: bfloat16 [8192, 8192], P('tensor', 'cache'), may hold values from -1 to 1
Outputs:
- attn_out: bfloat16 [256, 4, 8192], P('tensor', None, 'cache')
The draws below stay inside these ranges and needn't reach their ends.
Inputs may be any that keep to these rules, and one draw needn't show every extreme that they name: `branch_prompt`: among the 8 rows of one cache index no prompt is named more than 2 times, a bound that some block reaches. `suffix_len`: some branch has a full suffix and some a suffix of one token.
All inputs are finite; a program needn't handle non-finite values.
Results may differ from the reference program's by a relative error of at most 0.01745.
Values may be sent and summed in bfloat16 or wider, within the bound.
No kernel may reach another device: no remote copies, remote signals or barrier semaphores. Data moves between devices by JAX's collectives and lax.ppermute only.
A program may use at most 64 MiB of HBM per device.

```python
import math
import jax
import jax.numpy as jnp
import numpy as np
from jax import lax

D = 8192
HEADS = 64
KV_HEADS = 8
HEAD_DIM = 128
PROMPT_LEN = 24576
STEPS = 4
BR_DEV = 8
SUFFIX = 512
PROMPTS = 8
CAP = 2
BRANCHES = 256
PREFIX = 196608
Q_WIDTH = 8192
KV_WIDTH = 1024


def draw_queries(key, part):
    key = jax.random.fold_in(key, 11)
    shape = (BRANCHES, STEPS, HEADS, HEAD_DIM)
    field = jnp.clip(2.0 * jax.random.normal(key, shape, jnp.float32), -12.0, 12.0)
    return field.reshape(BRANCHES, STEPS, HEADS * HEAD_DIM).astype(jnp.bfloat16)


def draw_prefix_kv(key, part):
    key = jax.random.fold_in(key, 21)
    shape = (2, PREFIX, KV_HEADS, HEAD_DIM)
    field = jnp.clip(jax.random.normal(key, shape, jnp.float32), -6.0, 6.0)
    return field.reshape(2, PREFIX, KV_HEADS * HEAD_DIM).astype(jnp.bfloat16)


def draw_suffix_kv(key, part):
    key = jax.random.fold_in(key, 31)
    shape = (BRANCHES, 2, SUFFIX, KV_HEADS, HEAD_DIM)
    spread = jnp.array([1.5, 1.0], jnp.float32)[None, :, None, None, None]
    field = jnp.clip(spread * jax.random.normal(key, shape, jnp.float32), -9.0, 9.0)
    return field.reshape(BRANCHES, 2, SUFFIX, KV_HEADS * HEAD_DIM).astype(jnp.bfloat16)


def draw_suffix_len(key, part):
    key = jax.random.fold_in(key, 41)
    lengths = jax.random.randint(key, (BRANCHES,), 1, SUFFIX + 1)
    full = jax.random.randint(jax.random.fold_in(key, 42), (), 0, BRANCHES)
    short = (full + 1 + jax.random.randint(jax.random.fold_in(key, 43), (), 0, BRANCHES - 1)) % BRANCHES
    lengths = lengths.at[full].set(SUFFIX).at[short].set(1)
    return lengths.astype(jnp.int32)


def steps_of(key, shape, shards, least, top_value):
    gain = 1.0
    for axis_at, blocks in shards:
        heights = jax.random.uniform(jax.random.fold_in(jax.random.fold_in(key, 6), axis_at), (blocks,), jnp.float32, least / len(shards), top_value / len(shards))
        gain = gain * jnp.repeat(jnp.exp(heights), shape[axis_at] // blocks).reshape((-1,) + (1,) * (len(shape) - 1 - axis_at))
    return gain


def routed_block(own_key, own, number, rows, number_of, top, most, slope):
    sequence = jax.random.permutation(own_key, number_of)
    packed, ordinary = portions_of(number_of, rows * top, most, slope, True), portions_of(number_of, rows * top, most, slope, False)
    places = jnp.arange(number_of)

    def named(tallies, rotation):
        used = int((tallies > 0).sum())
        fixed = max(1, used // 4)
        shifted = fixed + (places - fixed + rotation * (used - fixed)) % max(1, number_of - fixed)
        return jnp.zeros((number_of,), jnp.int32).at[sequence[jnp.where(places < fixed, places, shifted)]].set(jnp.asarray(tallies, jnp.int32))

    tallies = jnp.where(number % 4 == 0, named(packed, number // 4), named(ordinary, number - number // 4 - 1))
    mixed = jax.random.permutation(jax.random.fold_in(own, 3), number_of)
    source_of, taker = mixed[0:number_of // 2 * 2:2], mixed[1:number_of // 2 * 2:2]
    slack = jnp.minimum(tallies[source_of] - 1, most - tallies[taker]) // 2
    slack = jnp.where((source_of == sequence[0]) | (taker == sequence[0]) | (tallies[taker] == 0), 0, jnp.maximum(slack, 0))
    shifted = jax.random.randint(jax.random.fold_in(own, 4), (number_of // 2,), 0, 1 << 20) % (slack + 1)
    tallies = tallies.at[source_of].add(-shifted).at[taker].add(shifted)
    members = jnp.searchsorted(jnp.cumsum(tallies), jnp.arange(rows * top), side="right").astype(jnp.int32)
    grid = members.reshape(top, rows).T
    grid = grid[jax.random.permutation(jax.random.fold_in(own, 1), rows)]
    rotation = jax.random.randint(jax.random.fold_in(own, 2), (rows, 1), 0, top)
    return jnp.take_along_axis(grid, (jnp.arange(top)[None, :] + rotation) % top, axis=1)


def portions_of(count, total, most, lean, full):
    portions = [(1 << 20) // math.isqrt(grade ** lean) + 1 for grade in range(1, count + 1)]
    largest = most if full else min(most, max(-(-total // count), total * portions[0] // sum(portions)))
    least = 1 if total - largest >= count - 1 else 0
    holding, surplus = [largest] + [least] * (count - 1), total - largest - least * (count - 1)
    while surplus > 0:
        candidates = [i for i in range(1, count) if holding[i] < largest] or [i for i in range(1, count) if holding[i] < most]
        pool, remaining = sum([portions[i] for i in candidates]), surplus
        for i in candidates:
            extra = min(most - holding[i], max(1, remaining * portions[i] // pool), surplus)
            holding[i] = holding[i] + extra
            surplus = surplus - extra
    return np.array(holding)


def gaussian(rng, extent, deviation, most, cuts=(), kind=jnp.bfloat16):
    values = jax.random.normal(rng, extent, jnp.float32) * deviation
    if len(cuts) > 0:
        values = steps_of(rng, extent, cuts, -0.22, 0.18) * values
    return jnp.clip(values, min=-most, max=most).astype(kind)


def setup_inputs(seed: int = 0) -> dict:
    splits = jax.random.split(jax.random.key(seed), 8)
    queries = draw_queries(jax.random.fold_in(splits[7], 71), 0)
    new_kv = gaussian(splits[1], (BRANCHES, STEPS, 2, KV_WIDTH), 2.0, 12.0, ((0, 32), (3, 8)))
    prefix_kv = draw_prefix_kv(jax.random.fold_in(splits[7], 71), 0)
    suffix_kv = draw_suffix_kv(jax.random.fold_in(splits[7], 71), 0)
    suffix_len = draw_suffix_len(jax.random.fold_in(splits[7], 71), 0)
    branch_prompt_keys = jax.random.split(jax.random.fold_in(splits[5], 1), BRANCHES // BR_DEV)
    branch_prompt_turns = jax.random.permutation(jax.random.fold_in(splits[5], 3), BRANCHES // BR_DEV)
    branch_prompt = jax.vmap(lambda own, number: routed_block(jax.random.fold_in(splits[5], 2), own, number, BR_DEV, PROMPTS, 1, CAP, 2))(branch_prompt_keys, branch_prompt_turns).reshape((BRANCHES, 1))
    out_weight = gaussian(splits[6], (Q_WIDTH, D), (Q_WIDTH // 256) ** -0.5, 1.0, ((0, 8), (1, 32)))
    return dict(queries=queries, new_kv=new_kv, prefix_kv=prefix_kv, suffix_kv=suffix_kv, suffix_len=suffix_len, branch_prompt=branch_prompt, out_weight=out_weight)


def reference(queries, new_kv, prefix_kv, suffix_kv, suffix_len, branch_prompt, out_weight):
    group = HEADS // KV_HEADS
    scale = HEAD_DIM ** -0.5
    reach = PROMPT_LEN + SUFFIX + STEPS

    def one_branch(item):
        query, fresh, suffix, length, prompt = item
        query_heads = query.reshape(STEPS, KV_HEADS, group, HEAD_DIM).astype(jnp.float32)
        start = (prompt * PROMPT_LEN).astype(jnp.int32)
        prompt_keys = lax.dynamic_slice_in_dim(prefix_kv[0], start, PROMPT_LEN, 0)
        prompt_values = lax.dynamic_slice_in_dim(prefix_kv[1], start, PROMPT_LEN, 0)
        keys = jnp.concatenate([prompt_keys, suffix[0], fresh[:, 0]], 0)
        values = jnp.concatenate([prompt_values, suffix[1], fresh[:, 1]], 0)
        keys = keys.reshape(reach, KV_HEADS, HEAD_DIM).astype(jnp.float32)
        values = values.reshape(reach, KV_HEADS, HEAD_DIM).astype(jnp.float32)
        scores = jnp.einsum('sghd,jgd->sghj', query_heads, keys) * scale
        place = jnp.arange(reach)
        steps = jnp.arange(STEPS)
        live = (place < PROMPT_LEN)[None, :] | ((place >= PROMPT_LEN) & (place < PROMPT_LEN + length))[None, :]
        live = live | ((place >= PROMPT_LEN + SUFFIX)[None, :] & ((place - PROMPT_LEN - SUFFIX)[None, :] <= steps[:, None]))
        scores = jnp.where(live[:, None, None, :], scores, -jnp.inf)
        top = jnp.max(scores, axis=-1, keepdims=True)
        weights = jnp.exp(scores - top)
        total = jnp.sum(weights, axis=-1)
        rounded = lax.optimization_barrier(weights.astype(jnp.bfloat16)).astype(jnp.float32)
        acc = jnp.einsum('sghj,jgd->sghd', rounded, values)
        return (acc / total[..., None]).astype(jnp.bfloat16).reshape(STEPS, HEADS * HEAD_DIM)

    mixed = lax.map(one_branch, (queries, new_kv, suffix_kv, suffix_len, branch_prompt[:, 0]))
    rows = mixed.reshape(BRANCHES * STEPS, HEADS * HEAD_DIM)
    result = jnp.dot(rows, out_weight, preferred_element_type=jnp.float32).astype(jnp.bfloat16)
    return result.reshape(BRANCHES, STEPS, D)
```

```python
import functools

import jax
import jax.numpy as jnp
from jax import lax
from jax.experimental import pallas as pl
from jax.experimental.pallas import tpu as pltpu
from jax.sharding import PartitionSpec as P

HEAD_DIM = 128
PROMPT_LEN = 24576
PROMPTS = 8
SLOTS = 2
LOG2E = 1.4426950408889634
SCORE = LOG2E * HEAD_DIM ** (-0.5)
VMEM_LIMIT = 48 * 1024 * 1024
F32 = jnp.float32
BF16 = jnp.bfloat16


def params():
    return pltpu.CompilerParams(vmem_limit_bytes=VMEM_LIMIT)


def whole(memory_space=pltpu.VMEM):
    return pl.BlockSpec(memory_space=memory_space)


def rank_of(prompt_ref, b):
    rank = jnp.int32(0)
    for earlier in range(b):
        rank += (prompt_ref[earlier] == prompt_ref[b]).astype(jnp.int32)
    return rank


def three_terms(value):
    high = value.astype(BF16).astype(F32)
    rest = value - high
    middle = rest.astype(BF16).astype(F32)
    return high, middle, rest - middle


def pack_kernel(branches, steps, group, prompt_ref, q_ref, packed_ref, rows_ref):
    height = steps * group
    packed_ref[...] = jnp.zeros_like(packed_ref)
    q = q_ref[...].astype(F32)
    for b in range(branches):
        own = q[b * steps : (b + 1) * steps]
        rows = jnp.concatenate(
            [own[:, h * HEAD_DIM : (h + 1) * HEAD_DIM] for h in range(group)], axis=0
        ).astype(BF16)
        rows_ref[b] = rows
        at = pl.multiple_of(rank_of(prompt_ref, b) * height, height)
        packed_ref[prompt_ref[b], pl.ds(at, height), :] = rows


def pack(prompt_ids, queries, group):
    branches, steps, _ = queries.shape
    height = steps * group
    return pl.pallas_call(
        functools.partial(pack_kernel, branches, steps, group),
        in_specs=[whole(pltpu.SMEM), whole()],
        out_specs=[whole(), whole()],
        out_shape=[
            jax.ShapeDtypeStruct((PROMPTS, SLOTS * height, HEAD_DIM), BF16),
            jax.ShapeDtypeStruct((branches, height, HEAD_DIM), BF16),
        ],
        compiler_params=params(),
        name="pack_queries",
    )(prompt_ids, queries.reshape(branches * steps, -1))


def attend_kernel(last, part, q_ref, kv_ref, out_ref, qt_ref, top_ref, total_ref, acc_ref):
    i = pl.program_id(0)
    rows = q_ref.shape[0]

    @pl.when(i == 0)
    def _():
        qt_ref[...] = q_ref[...].T
        top_ref[...] = jnp.full(top_ref.shape, -jnp.inf, F32)
        total_ref[...] = jnp.zeros(total_ref.shape, F32)
        acc_ref[...] = jnp.zeros(acc_ref.shape, F32)

    top, total, acc = top_ref[...], total_ref[...], acc_ref[...]
    for k in range(0, kv_ref.shape[1], part):
        scores = jnp.dot(kv_ref[0, k : k + part, :], qt_ref[...], preferred_element_type=F32)
        new_top = jnp.maximum(top, jnp.max(scores, axis=0, keepdims=True))
        weights = jnp.exp2((scores - new_top) * SCORE)
        fade = jnp.exp2((top - new_top) * SCORE)
        total = total * fade + jnp.sum(weights, axis=0, keepdims=True)
        acc = acc * fade + lax.dot_general(
            kv_ref[1, k : k + part, :],
            weights.astype(BF16),
            (((0,), (0,)), ((), ())),
            preferred_element_type=F32,
        )
        top = new_top
    top_ref[...], total_ref[...], acc_ref[...] = top, total, acc

    @pl.when(i == last)
    def _():
        total = total_ref[...]
        out_ref[0:HEAD_DIM, :] = (acc_ref[...] / total).astype(BF16)
        terms = three_terms(top_ref[...] * SCORE + jnp.log2(total))
        row = lax.broadcasted_iota(jnp.int32, (16, rows), 0)
        stats = jnp.zeros((16, rows), F32)
        for j in range(3):
            stats = jnp.where(row == j, terms[j], stats)
        out_ref[HEAD_DIM : HEAD_DIM + 16, :] = stats.astype(BF16)


def attend(q, kv):
    rows, length = q.shape[0], kv.shape[1]
    block, part = 2048, 1024
    return pl.pallas_call(
        functools.partial(attend_kernel, length // block - 1, part),
        grid=(length // block,),
        in_specs=[
            pl.BlockSpec((rows, HEAD_DIM), lambda i: (0, 0)),
            pl.BlockSpec((2, block, HEAD_DIM), lambda i: (0, i, 0)),
        ],
        out_specs=pl.BlockSpec((HEAD_DIM + 16, rows), lambda i: (0, 0)),
        out_shape=jax.ShapeDtypeStruct((HEAD_DIM + 16, rows), BF16),
        scratch_shapes=[
            pltpu.VMEM((HEAD_DIM, rows), BF16),
            pltpu.VMEM((1, rows), F32),
            pltpu.VMEM((1, rows), F32),
            pltpu.VMEM((HEAD_DIM, rows), F32),
        ],
        compiler_params=params(),
        cost_estimate=pl.CostEstimate(
            flops=8 * rows * length * HEAD_DIM,
            transcendentals=rows * length,
            bytes_accessed=4 * length * HEAD_DIM,
        ),
        name="prefix_attention",
    )(q, kv)


def suffix_kernel(steps, len_ref, q_ref, kv_ref, new_ref, out_ref, lse_ref):
    length = len_ref[pl.program_id(0)]
    slots = kv_ref.shape[2]
    keys = jnp.concatenate([kv_ref[0, 0], new_ref[0, 0]], axis=0)
    values = jnp.concatenate([kv_ref[0, 1], new_ref[0, 1]], axis=0)
    scores = lax.dot_general(
        q_ref[0], keys, (((1,), (1,)), ((), ())), preferred_element_type=F32
    )
    place = lax.broadcasted_iota(jnp.int32, scores.shape, 1)
    step = lax.broadcasted_iota(jnp.int32, scores.shape, 0) % steps
    live = (place < length) | ((place >= slots) & (place - slots <= step))
    scores = jnp.where(live, scores, -jnp.inf)
    top = jnp.max(scores, axis=1, keepdims=True)
    weights = jnp.exp2((scores - top) * SCORE)
    total = jnp.sum(weights, axis=1, keepdims=True)
    acc = jnp.dot(weights.astype(BF16), values, preferred_element_type=F32)
    out_ref[0] = acc / total
    lse_ref[0] = jnp.broadcast_to(top * SCORE + jnp.log2(total), acc.shape)


def suffix(lengths, q_rows, suffix_kv, fresh, steps):
    branches, height, _ = q_rows.shape
    block = pl.BlockSpec((1, height, HEAD_DIM), lambda i: (i, 0, 0))
    return pl.pallas_call(
        functools.partial(suffix_kernel, steps),
        grid=(branches,),
        in_specs=[
            whole(pltpu.SMEM),
            block,
            pl.BlockSpec((1,) + suffix_kv.shape[1:], lambda i: (i, 0, 0, 0)),
            pl.BlockSpec((1,) + fresh.shape[1:], lambda i: (i, 0, 0, 0)),
        ],
        out_specs=[block, block],
        out_shape=[jax.ShapeDtypeStruct((branches, height, HEAD_DIM), F32)] * 2,
        compiler_params=params(),
        name="suffix_attention",
    )(lengths, q_rows, suffix_kv, fresh)


def merge_kernel(homes, *refs):
    *part_refs, out_ref = refs
    parts = [ref[...].astype(F32) for ref in part_refs]
    lses = [jnp.sum(p[HEAD_DIM : HEAD_DIM + 3], axis=0, keepdims=True) for p in parts]
    top = functools.reduce(jnp.maximum, lses)
    shares = [jnp.exp2(lse - top) for lse in lses]
    total = sum(shares)
    acc = sum(p[0:HEAD_DIM] * share for p, share in zip(parts, shares, strict=True))
    rows = acc.shape[1]
    height = rows // homes
    out_ref[:, 0:height, :] = (acc / total).T.astype(BF16).reshape(homes, height, HEAD_DIM)
    terms = three_terms(top + jnp.log2(total))
    row = lax.broadcasted_iota(jnp.int32, (16, rows), 0)
    stats = jnp.zeros((16, rows), F32)
    for j in range(3):
        stats = jnp.where(row == j, terms[j], stats)
    stats = stats.astype(BF16)
    for home in range(homes):
        at = home * height // HEAD_DIM * HEAD_DIM
        out_ref[home, height : height + 16, :] = stats[:, at : at + HEAD_DIM]


def merge(parts, homes):
    height = parts[0].shape[1] // homes
    return pl.pallas_call(
        functools.partial(merge_kernel, homes),
        in_specs=[whole()] * len(parts),
        out_specs=whole(),
        out_shape=jax.ShapeDtypeStruct((homes, height + 16, HEAD_DIM), BF16),
        compiler_params=params(),
        name="merge_parts",
    )(*parts)


def finish_kernel(steps, group, prompt_ref, home_ref, back_ref, own_ref, lse_ref, out_ref, col_ref):
    branches, height, _ = own_ref.shape
    tall = SLOTS * height
    lanes = (home_ref[0] * tall) % HEAD_DIM
    pieces = []
    for b in range(branches):
        prompt = prompt_ref[b]
        at = pl.multiple_of(rank_of(prompt_ref, b) * height, height)
        part = back_ref[prompt, pl.ds(at, height), :].astype(F32)
        stats = back_ref[prompt, tall : tall + 16, :].astype(F32)
        part_lse = jnp.sum(stats[0:3], axis=0, keepdims=True)
        col_ref[b] = jnp.broadcast_to(part_lse, (HEAD_DIM, HEAD_DIM)).T
        part_lse = col_ref[b, pl.ds(pl.multiple_of(lanes + at, height), height), :]
        own_lse = lse_ref[b]
        top = jnp.maximum(part_lse, own_lse)
        part_share = jnp.exp2(part_lse - top)
        own_share = jnp.exp2(own_lse - top)
        mixed = (part * part_share + own_ref[b] * own_share) / (part_share + own_share)
        pieces.append(
            jnp.concatenate([mixed[h * steps : (h + 1) * steps] for h in range(group)], axis=1)
        )
    out_ref[...] = jnp.concatenate(pieces, axis=0).astype(BF16)


def finish(prompt_ids, home, back, own, lse, steps, group):
    branches = own.shape[0]
    return pl.pallas_call(
        functools.partial(finish_kernel, steps, group),
        in_specs=[whole(pltpu.SMEM), whole(pltpu.SMEM), whole(), whole(), whole()],
        out_specs=whole(),
        out_shape=jax.ShapeDtypeStruct((branches * steps, group * HEAD_DIM), BF16),
        scratch_shapes=[pltpu.VMEM((branches, HEAD_DIM, HEAD_DIM), F32)],
        compiler_params=params(),
        name="finish_attention",
    )(prompt_ids, home, back, own, lse)


def project_kernel(place_ref, *refs):
    *mixed_refs, weight_ref, out_ref, rows_ref = refs
    count = len(mixed_refs)
    height = mixed_refs[0].shape[0]

    @pl.when(pl.program_id(0) == 0)
    def _():
        for k, ref in enumerate(mixed_refs):
            at = lax.rem(place_ref[0] + count - k, count) * height
            rows_ref[pl.ds(pl.multiple_of(at, height), height), :] = ref[...]

    out_ref[0] = jnp.dot(rows_ref[...], weight_ref[0], preferred_element_type=F32).astype(
        out_ref.dtype
    )


def project(place, mixed, weight, dtype):
    height, depth = mixed[0].shape
    blocks, _, width = weight.shape
    rows = height * len(mixed)
    return pl.pallas_call(
        project_kernel,
        grid_spec=pltpu.PrefetchScalarGridSpec(
            num_scalar_prefetch=1,
            grid=(blocks // 2,),
            in_specs=[pl.BlockSpec((height, depth), lambda i, place: (0, 0))] * len(mixed)
            + [pl.BlockSpec((1, depth, width), lambda i, place: (place[1] + i, 0, 0))],
            out_specs=pl.BlockSpec((1, rows, width), lambda i, place: (i, 0, 0)),
            scratch_shapes=[pltpu.VMEM((rows, depth), BF16)],
        ),
        out_shape=jax.ShapeDtypeStruct((blocks // 2, rows, width), dtype),
        compiler_params=params(),
        name="project",
    )(place, *mixed, weight)


def per_device(nz, nx, ny, queries, new_kv, prefix_kv, suffix_kv, suffix_len, branch_prompt, out_weight):
    branches, steps, qwidth = queries.shape
    group = qwidth // HEAD_DIM
    height = steps * group
    cache, tensor = lax.axis_index("cache"), lax.axis_index("tensor")
    x, core = cache % nx, tensor % 2
    z_groups = [[z * nx + i for z in range(nz)] for i in range(nx)]
    y_groups = [[y * 2 + c for y in range(ny)] for c in range(2)]

    def along_x(value, k):
        pairs = [(z * nx + i, z * nx + (i + k) % nx) for z in range(nz) for i in range(nx)]
        return lax.ppermute(value, "cache", pairs)

    prompt_ids = branch_prompt[:, 0]
    weight = lax.all_gather(out_weight, "cache", axis_index_groups=z_groups)
    packed, q_rows = pack(prompt_ids, queries, group)
    mine = lax.all_to_all(packed, "cache", 0, 0, axis_index_groups=z_groups, tiled=True)
    mine = mine.reshape(nz * SLOTS * height, HEAD_DIM)
    sent = [along_x(mine, k) for k in range(1, nx)]
    fresh = jnp.pad(new_kv.transpose(0, 2, 1, 3), ((0, 0), (0, 0), (0, 16 - steps), (0, 0)))
    own, own_lse = suffix(suffix_len, q_rows, suffix_kv, fresh, steps)
    parts = [attend(mine, prefix_kv)]
    for k in range(1, nx):
        parts.append(along_x(attend(sent[k - 1], prefix_kv), nx - k))
    merged = merge(parts, nz)
    back = lax.all_to_all(merged, "cache", 0, 0, axis_index_groups=z_groups, tiled=True)
    home = (cache // nx).reshape(1)
    mixed = finish(prompt_ids, home, back, own, own_lse, steps, group)
    plane = [mixed] + [along_x(mixed, k) for k in range(1, nx)]
    half = nz // 2
    theirs = project(jnp.stack([x, (1 - core) * half]), plane, weight, BF16)
    theirs = lax.ppermute(theirs, "tensor", [(t, t ^ 1) for t in range(2 * ny)])
    ours = project(jnp.stack([x, core * half]), plane, weight, F32)
    pair = (ours + theirs.astype(F32)).astype(BF16)
    column = lax.all_to_all(pair, "tensor", 0, 0, axis_index_groups=y_groups, tiled=True)
    column = jnp.sum(column.astype(F32), axis=0).astype(BF16)
    nt = 2 * ny
    pairs = [
        ((z * nx + i) * nt + y * 2 + c, ((c * half + y) * nx + i) * nt + z)
        for z in range(nz)
        for i in range(nx)
        for y in range(ny)
        for c in range(2)
    ]
    result = lax.ppermute(column, ("cache", "tensor"), pairs)
    return result.reshape(-1, steps, result.shape[-1])


def solution(mesh):
    ncache, ntensor = mesh.shape["cache"], mesh.shape["tensor"]
    nz = PROMPTS
    return jax.shard_map(
        functools.partial(per_device, nz, ncache // nz, ntensor // 2),
        mesh=mesh,
        in_specs=(
            P("cache", None, "tensor"),
            P("cache", None, None, "tensor"),
            P(None, "cache", "tensor"),
            P("cache", None, None, "tensor"),
            P("cache"),
            P("cache", None),
            P("tensor", "cache"),
        ),
        out_specs=P("tensor", None, "cache"),
        check_vma=False,
    )
```

```python
import functools

import jax
import jax.numpy as jnp
from jax import lax
from jax.experimental import pallas as pl
from jax.experimental.pallas import tpu as pltpu
from jax.sharding import PartitionSpec as P

HEAD_DIM = 128
PROMPT_LEN = 24576
PROMPTS = 8
SLOTS = 2
LOG2E = 1.4426950408889634
SCORE = LOG2E * HEAD_DIM ** (-0.5)
PART = 512
LARGE = 2.0**100
VMEM_LIMIT = 48 * 1024 * 1024
F32 = jnp.float32
BF16 = jnp.bfloat16


def params():
    return pltpu.CompilerParams(vmem_limit_bytes=VMEM_LIMIT)


def whole(memory_space=pltpu.VMEM):
    return pl.BlockSpec(memory_space=memory_space)


def rank_of(prompt_ref, b):
    rank = jnp.int32(0)
    for earlier in range(b):
        rank += (prompt_ref[earlier] == prompt_ref[b]).astype(jnp.int32)
    return rank


def three_terms(value):
    high = value.astype(BF16).astype(F32)
    rest = value - high
    middle = rest.astype(BF16).astype(F32)
    return high, middle, rest - middle


def pack_kernel(
    branches, steps, group, prompt_hbm, q_hbm, packed_ref, rows_ref, prompt_ref, q_ref, sem
):
    height = steps * group
    copies = [
        pltpu.make_async_copy(prompt_hbm, prompt_ref, sem.at[0]),
        pltpu.make_async_copy(q_hbm, q_ref, sem.at[1]),
    ]
    for copy in copies:
        copy.start()
    packed_ref[...] = jnp.zeros_like(packed_ref)
    for copy in copies:
        copy.wait()
    for b in range(branches):
        own = q_ref[b].astype(F32)
        rows = jnp.concatenate(
            [own[:, h * HEAD_DIM : (h + 1) * HEAD_DIM] for h in range(group)], axis=0
        ).astype(BF16)
        rows_ref[b] = rows
        at = pl.multiple_of(rank_of(prompt_ref, b) * height, height)
        packed_ref[prompt_ref[b], pl.ds(at, height), :] = rows


def pack(prompt_ids, queries, group):
    branches, steps, _ = queries.shape
    height = steps * group
    return pl.pallas_call(
        functools.partial(pack_kernel, branches, steps, group),
        in_specs=[whole(pltpu.HBM), whole(pltpu.HBM)],
        out_specs=[whole(), whole()],
        out_shape=[
            jax.ShapeDtypeStruct((PROMPTS, SLOTS * height, HEAD_DIM), BF16),
            jax.ShapeDtypeStruct((branches, height, HEAD_DIM), BF16),
        ],
        scratch_shapes=[
            pltpu.SMEM((branches,), jnp.int32),
            pltpu.VMEM(queries.shape, BF16),
            pltpu.SemaphoreType.DMA((2,)),
        ],
        compiler_params=params(),
        name="pack_queries",
    )(
        pltpu.with_memory_space_constraint(prompt_ids, pltpu.HBM),
        pltpu.with_memory_space_constraint(queries, pltpu.HBM),
    )


def attend_kernel(part, q_ref, kv_ref, out_ref, qt_ref, top_ref, total_ref, acc_ref):
    rows, length = q_ref.shape[0], kv_ref.shape[1]
    qt_ref[...] = q_ref[...].T

    def scores_of(k):
        return jnp.dot(kv_ref[0, pl.ds(k, part), :], qt_ref[...], preferred_element_type=F32)

    def sums_of(k, weights):
        return lax.dot_general(
            kv_ref[1, pl.ds(k, part), :],
            weights.astype(BF16),
            (((0,), (0,)), ((), ())),
            preferred_element_type=F32,
        )

    following = scores_of(0)
    top = jnp.max(following, axis=0, keepdims=True)
    total = jnp.zeros((8, rows), F32)
    acc = jnp.zeros((HEAD_DIM, rows), F32)
    for k in range(0, length, part):
        scores = following
        if k + part < length:
            following = scores_of(k + part)
        weights = jnp.exp2((scores - top) * SCORE)
        total = total + jnp.sum(weights.reshape(part // 8, 8, rows), axis=0)
        acc = acc + sums_of(k, weights)
    total = jnp.sum(total, axis=0, keepdims=True)
    top_ref[...], total_ref[...], acc_ref[...] = top, total, acc

    @pl.when(jnp.logical_not(jnp.max(total) < LARGE))
    def _():
        top_ref[...] = jnp.full((1, rows), -jnp.inf, F32)
        total_ref[...] = jnp.zeros((1, rows), F32)
        acc_ref[...] = jnp.zeros((HEAD_DIM, rows), F32)

        @pl.loop(0, length // part)
        def _(i):
            k = pl.multiple_of(i * part, part)
            scores = scores_of(k)
            top = top_ref[...]
            new_top = jnp.maximum(top, jnp.max(scores, axis=0, keepdims=True))
            weights = jnp.exp2((scores - new_top) * SCORE)
            fade = jnp.exp2((top - new_top) * SCORE)
            total_ref[...] = total_ref[...] * fade + jnp.sum(weights, axis=0, keepdims=True)
            acc_ref[...] = acc_ref[...] * fade + sums_of(k, weights)
            top_ref[...] = new_top

    total = total_ref[...]
    out_ref[0:HEAD_DIM, :] = (acc_ref[...] / total).astype(BF16)
    terms = three_terms(top_ref[...] * SCORE + jnp.log2(total))
    row = lax.broadcasted_iota(jnp.int32, (16, rows), 0)
    stats = jnp.zeros((16, rows), F32)
    for j in range(3):
        stats = jnp.where(row == j, terms[j], stats)
    out_ref[HEAD_DIM : HEAD_DIM + 16, :] = stats.astype(BF16)


def attend(q, kv):
    rows, length = q.shape[0], kv.shape[1]
    return pl.pallas_call(
        functools.partial(attend_kernel, PART),
        in_specs=[whole(), whole()],
        out_specs=whole(),
        out_shape=jax.ShapeDtypeStruct((HEAD_DIM + 16, rows), BF16),
        scratch_shapes=[
            pltpu.VMEM((HEAD_DIM, rows), BF16),
            pltpu.VMEM((1, rows), F32),
            pltpu.VMEM((1, rows), F32),
            pltpu.VMEM((HEAD_DIM, rows), F32),
        ],
        compiler_params=params(),
        cost_estimate=pl.CostEstimate(
            flops=8 * rows * length * HEAD_DIM,
            transcendentals=rows * length,
            bytes_accessed=4 * length * HEAD_DIM,
        ),
        name="prefix_attention",
    )(q, kv)


def suffix_kernel(steps, len_ref, q_ref, kv_ref, new_ref, out_ref, lse_ref):
    length = len_ref[pl.program_id(0)]
    slots = kv_ref.shape[2]
    keys = jnp.concatenate([kv_ref[0, 0], new_ref[0, 0]], axis=0)
    values = jnp.concatenate([kv_ref[0, 1], new_ref[0, 1]], axis=0)
    scores = lax.dot_general(
        q_ref[0], keys, (((1,), (1,)), ((), ())), preferred_element_type=F32
    )
    place = lax.broadcasted_iota(jnp.int32, scores.shape, 1)
    step = lax.broadcasted_iota(jnp.int32, scores.shape, 0) % steps
    live = (place < length) | ((place >= slots) & (place - slots <= step))
    scores = jnp.where(live, scores, -jnp.inf)
    top = jnp.max(scores, axis=1, keepdims=True)
    weights = jnp.exp2((scores - top) * SCORE)
    total = jnp.sum(weights, axis=1, keepdims=True)
    acc = jnp.dot(weights.astype(BF16), values, preferred_element_type=F32)
    out_ref[0] = acc / total
    lse_ref[0] = jnp.broadcast_to(top * SCORE + jnp.log2(total), acc.shape)


def suffix(lengths, q_rows, suffix_kv, fresh, steps):
    branches, height, _ = q_rows.shape
    block = pl.BlockSpec((1, height, HEAD_DIM), lambda i: (i, 0, 0))
    return pl.pallas_call(
        functools.partial(suffix_kernel, steps),
        grid=(branches,),
        in_specs=[
            whole(pltpu.SMEM),
            block,
            pl.BlockSpec((1,) + suffix_kv.shape[1:], lambda i: (i, 0, 0, 0)),
            pl.BlockSpec((1,) + fresh.shape[1:], lambda i: (i, 0, 0, 0)),
        ],
        out_specs=[block, block],
        out_shape=[jax.ShapeDtypeStruct((branches, height, HEAD_DIM), F32)] * 2,
        compiler_params=params(),
        name="suffix_attention",
    )(lengths, q_rows, suffix_kv, fresh)


def merge_kernel(homes, *refs):
    *part_refs, out_ref = refs
    parts = [ref[...].astype(F32) for ref in part_refs]
    lses = [jnp.sum(p[HEAD_DIM : HEAD_DIM + 3], axis=0, keepdims=True) for p in parts]
    top = functools.reduce(jnp.maximum, lses)
    shares = [jnp.exp2(lse - top) for lse in lses]
    total = sum(shares)
    acc = sum(p[0:HEAD_DIM] * share for p, share in zip(parts, shares, strict=True))
    rows = acc.shape[1]
    height = rows // homes
    out_ref[:, 0:height, :] = (acc / total).T.astype(BF16).reshape(homes, height, HEAD_DIM)
    terms = three_terms(top + jnp.log2(total))
    row = lax.broadcasted_iota(jnp.int32, (16, rows), 0)
    stats = jnp.zeros((16, rows), F32)
    for j in range(3):
        stats = jnp.where(row == j, terms[j], stats)
    stats = stats.astype(BF16)
    for home in range(homes):
        at = home * height // HEAD_DIM * HEAD_DIM
        out_ref[home, height : height + 16, :] = stats[:, at : at + HEAD_DIM]


def merge(parts, homes):
    height = parts[0].shape[1] // homes
    return pl.pallas_call(
        functools.partial(merge_kernel, homes),
        in_specs=[whole()] * len(parts),
        out_specs=whole(),
        out_shape=jax.ShapeDtypeStruct((homes, height + 16, HEAD_DIM), BF16),
        compiler_params=params(),
        name="merge_parts",
    )(*parts)


def finish_kernel(steps, group, prompt_ref, home_ref, back_ref, own_ref, lse_ref, out_ref, col_ref):
    branches, height, _ = own_ref.shape
    tall = SLOTS * height
    lanes = (home_ref[0] * tall) % HEAD_DIM
    pieces = []
    for b in range(branches):
        prompt = prompt_ref[b]
        at = pl.multiple_of(rank_of(prompt_ref, b) * height, height)
        part = back_ref[prompt, pl.ds(at, height), :].astype(F32)
        stats = back_ref[prompt, tall : tall + 16, :].astype(F32)
        part_lse = jnp.sum(stats[0:3], axis=0, keepdims=True)
        col_ref[b] = jnp.broadcast_to(part_lse, (HEAD_DIM, HEAD_DIM)).T
        part_lse = col_ref[b, pl.ds(pl.multiple_of(lanes + at, height), height), :]
        own_lse = lse_ref[b]
        top = jnp.maximum(part_lse, own_lse)
        part_share = jnp.exp2(part_lse - top)
        own_share = jnp.exp2(own_lse - top)
        mixed = (part * part_share + own_ref[b] * own_share) / (part_share + own_share)
        pieces.append(
            jnp.concatenate([mixed[h * steps : (h + 1) * steps] for h in range(group)], axis=1)
        )
    out_ref[...] = jnp.concatenate(pieces, axis=0).astype(BF16)


def finish(prompt_ids, home, back, own, lse, steps, group):
    branches = own.shape[0]
    return pl.pallas_call(
        functools.partial(finish_kernel, steps, group),
        in_specs=[whole(pltpu.SMEM), whole(pltpu.SMEM), whole(), whole(), whole()],
        out_specs=whole(),
        out_shape=jax.ShapeDtypeStruct((branches * steps, group * HEAD_DIM), BF16),
        scratch_shapes=[pltpu.VMEM((branches, HEAD_DIM, HEAD_DIM), F32)],
        compiler_params=params(),
        name="finish_attention",
    )(prompt_ids, home, back, own, lse)


def load_kernel(count, source_ref, out_ref, sem):
    size = source_ref.shape[0] // count
    copies = [
        pltpu.make_async_copy(
            source_ref.at[pl.ds(i * size, size)], out_ref.at[pl.ds(i * size, size)], sem.at[i]
        )
        for i in range(count)
    ]
    for copy in copies:
        copy.start()
    for copy in copies:
        copy.wait()


def load(value, count):
    return pl.pallas_call(
        functools.partial(load_kernel, count),
        in_specs=[whole(pl.ANY)],
        out_specs=whole(),
        out_shape=pltpu.VMEM(value.shape, value.dtype),
        scratch_shapes=[pltpu.SemaphoreType.DMA((count,))],
        compiler_params=params(),
        cost_estimate=pl.CostEstimate(
            flops=0, transcendentals=0, bytes_accessed=2 * value.size * value.dtype.itemsize
        ),
        name="load",
    )(value)


def project_kernel(place_ref, *refs):
    *mixed_refs, weight_ref, theirs_ref, ours_ref, rows_ref = refs
    count = len(mixed_refs)
    height = mixed_refs[0].shape[0]
    for k, ref in enumerate(mixed_refs):
        at = lax.rem(place_ref[0] + count - k, count) * height
        rows_ref[pl.ds(pl.multiple_of(at, height), height), :] = ref[...]
    half = ours_ref.shape[0]
    core, odd = place_ref[1], place_ref[2]
    for out_ref, first in ((theirs_ref, (1 - core) * half), (ours_ref, core * half)):
        for i in range(half):
            block = first + lax.rem(i + odd * (half // 2), half)
            out_ref[i] = jnp.dot(
                rows_ref[...], weight_ref[block], preferred_element_type=F32
            ).astype(out_ref.dtype)


def project(place, mixed, weight):
    height, depth = mixed[0].shape
    blocks, _, width = weight.shape
    rows = height * len(mixed)
    shape = (blocks // 2, rows, width)
    return pl.pallas_call(
        project_kernel,
        in_specs=[whole(pltpu.SMEM)] + [whole()] * (len(mixed) + 1),
        out_specs=[whole(), whole()],
        out_shape=[jax.ShapeDtypeStruct(shape, BF16), jax.ShapeDtypeStruct(shape, F32)],
        scratch_shapes=[pltpu.VMEM((rows, depth), BF16)],
        compiler_params=params(),
        name="project",
    )(place, *mixed, weight)


def sum_kernel(*refs):
    *piece_refs, out_ref = refs
    total = sum(ref[...].astype(F32) for ref in piece_refs)
    out_ref[...] = total.reshape(out_ref.shape).astype(BF16)


def sum_pieces(pieces, steps):
    rows, width = pieces[0].shape
    return pl.pallas_call(
        sum_kernel,
        in_specs=[whole()] * len(pieces),
        out_specs=whole(),
        out_shape=jax.ShapeDtypeStruct((rows // steps, steps, width), BF16),
        compiler_params=params(),
        name="sum_pieces",
    )(*pieces)


def per_device(nz, nx, ny, queries, new_kv, prefix_kv, suffix_kv, suffix_len, branch_prompt, out_weight):
    branches, steps, qwidth = queries.shape
    group = qwidth // HEAD_DIM
    height = steps * group
    cache, tensor = lax.axis_index("cache"), lax.axis_index("tensor")
    x, y, core = cache % nx, tensor // 2, tensor % 2
    z_groups = [[z * nx + i for z in range(nz)] for i in range(nx)]

    def along_x(value, k):
        pairs = [(z * nx + i, z * nx + (i + k) % nx) for z in range(nz) for i in range(nx)]
        return lax.ppermute(value, "cache", pairs)

    prompt_ids = branch_prompt[:, 0]
    packed, q_rows = pack(prompt_ids, queries, group)
    weight = lax.all_gather(out_weight, "cache", axis_index_groups=z_groups)
    mine = lax.all_to_all(packed, "cache", 0, 0, axis_index_groups=z_groups, tiled=True)
    kv = load(prefix_kv, 2)
    mine, kv = lax.optimization_barrier((mine, kv))
    mine = mine.reshape(nz * SLOTS * height, HEAD_DIM)
    sent = [along_x(mine, k) for k in range(1, nx)]
    fresh = jnp.pad(new_kv.transpose(0, 2, 1, 3), ((0, 0), (0, 0), (0, 16 - steps), (0, 0)))
    own, own_lse = suffix(suffix_len, q_rows, suffix_kv, fresh, steps)
    parts = [attend(mine, kv)]
    for k in range(1, nx):
        parts.append(along_x(attend(sent[k - 1], kv), nx - k))
    merged = merge(parts, nz)
    back = lax.all_to_all(merged, "cache", 0, 0, axis_index_groups=z_groups, tiled=True)
    home = (cache // nx).reshape(1)
    mixed = finish(prompt_ids, home, back, own, own_lse, steps, group)
    plane = [mixed] + [along_x(mixed, k) for k in range(1, nx)]
    half = nz // 2
    theirs, ours = project(jnp.stack([x, core, y % 2]), plane, load(weight, nz))
    theirs = lax.ppermute(theirs, "tensor", [(t, t ^ 1) for t in range(2 * ny)])
    keep = ours[:2] + theirs[:2].astype(F32)
    give = (ours[2:] + theirs[2:].astype(F32)).astype(BF16)
    keep = (keep + lax.ppermute(give, "tensor", [(t, t ^ 2) for t in range(2 * ny)])).astype(BF16)
    pieces = []
    for k in range(2):
        pairs = [
            (
                ((z * nx + i) * ny + j) * 2 + c,
                ((c * half + (j % 2) * 2 + (k + j // 2) % 2) * nx + i) * 2 * ny + z,
            )
            for z in range(nz)
            for i in range(nx)
            for j in range(ny)
            for c in range(2)
        ]
        block = lax.dynamic_index_in_dim(keep, (k + y // 2) % 2, 0, keepdims=False)
        pieces.append(lax.ppermute(block, ("cache", "tensor"), pairs))
    return sum_pieces(pieces, steps)


def solution(mesh):
    ncache, ntensor = mesh.shape["cache"], mesh.shape["tensor"]
    nz = PROMPTS
    return jax.shard_map(
        functools.partial(per_device, nz, ncache // nz, ntensor // 2),
        mesh=mesh,
        in_specs=(
            P("cache", None, "tensor"),
            P("cache", None, None, "tensor"),
            P(None, "cache", "tensor"),
            P("cache", None, None, "tensor"),
            P("cache"),
            P("cache", None),
            P("tensor", "cache"),
        ),
        out_specs=P("tensor", None, "cache"),
        check_vma=False,
    )
```

```python
import functools

import jax
import jax.numpy as jnp
from jax import lax
from jax.experimental import pallas as pl
from jax.experimental.pallas import tpu as pltpu
from jax.sharding import PartitionSpec as P

HEAD_DIM = 128
PROMPT_LEN = 24576
PROMPTS = 8
SLOTS = 2
LOG2E = 1.4426950408889634
SCORE = LOG2E * HEAD_DIM ** (-0.5)
PART = 512
LARGE = 2.0**100
VMEM_LIMIT = 48 * 1024 * 1024
F32 = jnp.float32
BF16 = jnp.bfloat16


def params():
    return pltpu.CompilerParams(vmem_limit_bytes=VMEM_LIMIT)


def whole(memory_space=pltpu.VMEM):
    return pl.BlockSpec(memory_space=memory_space)


def rank_of(prompt_ref, b):
    rank = jnp.int32(0)
    for earlier in range(b):
        rank += (prompt_ref[earlier] == prompt_ref[b]).astype(jnp.int32)
    return rank


def three_terms(value):
    high = value.astype(BF16).astype(F32)
    rest = value - high
    middle = rest.astype(BF16).astype(F32)
    return high, middle, rest - middle


def pack_kernel(
    branches, steps, group, prompt_hbm, q_hbm, packed_ref, rows_ref, prompt_ref, q_ref, sem
):
    height = steps * group
    copies = [
        pltpu.make_async_copy(prompt_hbm, prompt_ref, sem.at[0]),
        pltpu.make_async_copy(q_hbm, q_ref, sem.at[1]),
    ]
    for copy in copies:
        copy.start()
    packed_ref[...] = jnp.zeros_like(packed_ref)
    for copy in copies:
        copy.wait()
    for b in range(branches):
        own = q_ref[b].astype(F32)
        rows = jnp.concatenate(
            [own[:, h * HEAD_DIM : (h + 1) * HEAD_DIM] for h in range(group)], axis=0
        ).astype(BF16)
        rows_ref[b] = rows
        at = pl.multiple_of(rank_of(prompt_ref, b) * height, height)
        packed_ref[prompt_ref[b], pl.ds(at, height), :] = rows


def pack(prompt_ids, queries, group):
    branches, steps, _ = queries.shape
    height = steps * group
    return pl.pallas_call(
        functools.partial(pack_kernel, branches, steps, group),
        in_specs=[whole(pltpu.HBM), whole(pltpu.HBM)],
        out_specs=[whole(), whole()],
        out_shape=[
            jax.ShapeDtypeStruct((PROMPTS, SLOTS * height, HEAD_DIM), BF16),
            jax.ShapeDtypeStruct((branches, height, HEAD_DIM), BF16),
        ],
        scratch_shapes=[
            pltpu.SMEM((branches,), jnp.int32),
            pltpu.VMEM(queries.shape, BF16),
            pltpu.SemaphoreType.DMA((2,)),
        ],
        compiler_params=params(),
        name="pack_queries",
    )(
        pltpu.with_memory_space_constraint(prompt_ids, pltpu.HBM),
        pltpu.with_memory_space_constraint(queries, pltpu.HBM),
    )


def attend_kernel(part, q_ref, kv_ref, out_ref, qt_ref, top_ref, total_ref, acc_ref):
    rows, length = q_ref.shape[0], kv_ref.shape[1]
    qt_ref[...] = q_ref[...].T

    def scores_of(k):
        return jnp.dot(kv_ref[0, pl.ds(k, part), :], qt_ref[...], preferred_element_type=F32)

    def sums_of(k, weights):
        return lax.dot_general(
            kv_ref[1, pl.ds(k, part), :],
            weights.astype(BF16),
            (((0,), (0,)), ((), ())),
            preferred_element_type=F32,
        )

    following = scores_of(0)
    top = jnp.max(following, axis=0, keepdims=True)
    total = jnp.zeros((8, rows), F32)
    acc = jnp.zeros((HEAD_DIM, rows), F32)
    for k in range(0, length, part):
        scores = following
        if k + part < length:
            following = scores_of(k + part)
        weights = jnp.exp2((scores - top) * SCORE)
        total = total + jnp.sum(weights.reshape(part // 8, 8, rows), axis=0)
        acc = acc + sums_of(k, weights)
    total = jnp.sum(total, axis=0, keepdims=True)
    top_ref[...], total_ref[...], acc_ref[...] = top, total, acc

    @pl.when(jnp.logical_not(jnp.max(total) < LARGE))
    def _():
        top_ref[...] = jnp.full((1, rows), -jnp.inf, F32)
        total_ref[...] = jnp.zeros((1, rows), F32)
        acc_ref[...] = jnp.zeros((HEAD_DIM, rows), F32)

        @pl.loop(0, length // part)
        def _(i):
            k = pl.multiple_of(i * part, part)
            scores = scores_of(k)
            top = top_ref[...]
            new_top = jnp.maximum(top, jnp.max(scores, axis=0, keepdims=True))
            weights = jnp.exp2((scores - new_top) * SCORE)
            fade = jnp.exp2((top - new_top) * SCORE)
            total_ref[...] = total_ref[...] * fade + jnp.sum(weights, axis=0, keepdims=True)
            acc_ref[...] = acc_ref[...] * fade + sums_of(k, weights)
            top_ref[...] = new_top

    total = total_ref[...]
    out_ref[0:HEAD_DIM, :] = (acc_ref[...] / total).astype(BF16)
    terms = three_terms(top_ref[...] * SCORE + jnp.log2(total))
    row = lax.broadcasted_iota(jnp.int32, (16, rows), 0)
    stats = jnp.zeros((16, rows), F32)
    for j in range(3):
        stats = jnp.where(row == j, terms[j], stats)
    out_ref[HEAD_DIM : HEAD_DIM + 16, :] = stats.astype(BF16)


def attend(q, kv):
    rows, length = q.shape[0], kv.shape[1]
    return pl.pallas_call(
        functools.partial(attend_kernel, PART),
        in_specs=[whole(), whole()],
        out_specs=whole(),
        out_shape=jax.ShapeDtypeStruct((HEAD_DIM + 16, rows), BF16),
        scratch_shapes=[
            pltpu.VMEM((HEAD_DIM, rows), BF16),
            pltpu.VMEM((1, rows), F32),
            pltpu.VMEM((1, rows), F32),
            pltpu.VMEM((HEAD_DIM, rows), F32),
        ],
        compiler_params=params(),
        cost_estimate=pl.CostEstimate(
            flops=8 * rows * length * HEAD_DIM,
            transcendentals=rows * length,
            bytes_accessed=4 * length * HEAD_DIM,
        ),
        name="prefix_attention",
    )(q, kv)


def suffix_kernel(steps, len_ref, q_ref, kv_ref, new_ref, out_ref, lse_ref):
    length = len_ref[pl.program_id(0)]
    slots = kv_ref.shape[2]
    keys = jnp.concatenate([kv_ref[0, 0], new_ref[0, 0]], axis=0)
    values = jnp.concatenate([kv_ref[0, 1], new_ref[0, 1]], axis=0)
    scores = lax.dot_general(
        q_ref[0], keys, (((1,), (1,)), ((), ())), preferred_element_type=F32
    )
    place = lax.broadcasted_iota(jnp.int32, scores.shape, 1)
    step = lax.broadcasted_iota(jnp.int32, scores.shape, 0) % steps
    live = (place < length) | ((place >= slots) & (place - slots <= step))
    scores = jnp.where(live, scores, -jnp.inf)
    top = jnp.max(scores, axis=1, keepdims=True)
    weights = jnp.exp2((scores - top) * SCORE)
    total = jnp.sum(weights, axis=1, keepdims=True)
    acc = jnp.dot(weights.astype(BF16), values, preferred_element_type=F32)
    out_ref[0] = acc / total
    lse_ref[0] = jnp.broadcast_to(top * SCORE + jnp.log2(total), acc.shape)


def suffix(lengths, q_rows, suffix_kv, fresh, steps):
    branches, height, _ = q_rows.shape
    block = pl.BlockSpec((1, height, HEAD_DIM), lambda i: (i, 0, 0))
    return pl.pallas_call(
        functools.partial(suffix_kernel, steps),
        grid=(branches,),
        in_specs=[
            whole(pltpu.SMEM),
            block,
            pl.BlockSpec((1,) + suffix_kv.shape[1:], lambda i: (i, 0, 0, 0)),
            pl.BlockSpec((1,) + fresh.shape[1:], lambda i: (i, 0, 0, 0)),
        ],
        out_specs=[block, block],
        out_shape=[jax.ShapeDtypeStruct((branches, height, HEAD_DIM), F32)] * 2,
        compiler_params=params(),
        name="suffix_attention",
    )(lengths, q_rows, suffix_kv, fresh)


def merge_kernel(homes, *refs):
    *part_refs, out_ref = refs
    parts = [ref[...].astype(F32) for ref in part_refs]
    lses = [jnp.sum(p[HEAD_DIM : HEAD_DIM + 3], axis=0, keepdims=True) for p in parts]
    top = functools.reduce(jnp.maximum, lses)
    shares = [jnp.exp2(lse - top) for lse in lses]
    total = sum(shares)
    acc = sum(p[0:HEAD_DIM] * share for p, share in zip(parts, shares, strict=True))
    rows = acc.shape[1]
    height = rows // homes
    out_ref[:, 0:height, :] = (acc / total).T.astype(BF16).reshape(homes, height, HEAD_DIM)
    terms = three_terms(top + jnp.log2(total))
    row = lax.broadcasted_iota(jnp.int32, (16, rows), 0)
    stats = jnp.zeros((16, rows), F32)
    for j in range(3):
        stats = jnp.where(row == j, terms[j], stats)
    stats = stats.astype(BF16)
    for home in range(homes):
        at = home * height // HEAD_DIM * HEAD_DIM
        out_ref[home, height : height + 16, :] = stats[:, at : at + HEAD_DIM]


def merge(parts, homes):
    height = parts[0].shape[1] // homes
    return pl.pallas_call(
        functools.partial(merge_kernel, homes),
        in_specs=[whole()] * len(parts),
        out_specs=whole(),
        out_shape=jax.ShapeDtypeStruct((homes, height + 16, HEAD_DIM), BF16),
        compiler_params=params(),
        name="merge_parts",
    )(*parts)


def finish_kernel(steps, group, prompt_ref, home_ref, back_ref, own_ref, lse_ref, out_ref, col_ref):
    branches, height, _ = own_ref.shape
    tall = SLOTS * height
    lanes = (home_ref[0] * tall) % HEAD_DIM
    pieces = []
    for b in range(branches):
        prompt = prompt_ref[b]
        at = pl.multiple_of(rank_of(prompt_ref, b) * height, height)
        part = back_ref[prompt, pl.ds(at, height), :].astype(F32)
        stats = back_ref[prompt, tall : tall + 16, :].astype(F32)
        part_lse = jnp.sum(stats[0:3], axis=0, keepdims=True)
        col_ref[b] = jnp.broadcast_to(part_lse, (HEAD_DIM, HEAD_DIM)).T
        part_lse = col_ref[b, pl.ds(pl.multiple_of(lanes + at, height), height), :]
        own_lse = lse_ref[b]
        top = jnp.maximum(part_lse, own_lse)
        part_share = jnp.exp2(part_lse - top)
        own_share = jnp.exp2(own_lse - top)
        mixed = (part * part_share + own_ref[b] * own_share) / (part_share + own_share)
        pieces.append(
            jnp.concatenate([mixed[h * steps : (h + 1) * steps] for h in range(group)], axis=1)
        )
    out_ref[...] = jnp.concatenate(pieces, axis=0).astype(BF16)


def finish(prompt_ids, home, back, own, lse, steps, group):
    branches = own.shape[0]
    return pl.pallas_call(
        functools.partial(finish_kernel, steps, group),
        in_specs=[whole(pltpu.SMEM), whole(pltpu.SMEM), whole(), whole(), whole()],
        out_specs=whole(),
        out_shape=jax.ShapeDtypeStruct((branches * steps, group * HEAD_DIM), BF16),
        scratch_shapes=[pltpu.VMEM((branches, HEAD_DIM, HEAD_DIM), F32)],
        compiler_params=params(),
        name="finish_attention",
    )(prompt_ids, home, back, own, lse)


def load_kernel(count, source_ref, out_ref, sem):
    size = source_ref.shape[0] // count
    copies = [
        pltpu.make_async_copy(
            source_ref.at[pl.ds(i * size, size)], out_ref.at[pl.ds(i * size, size)], sem.at[i]
        )
        for i in range(count)
    ]
    for copy in copies:
        copy.start()
    for copy in copies:
        copy.wait()


def load(value, count):
    return pl.pallas_call(
        functools.partial(load_kernel, count),
        in_specs=[whole(pl.ANY)],
        out_specs=whole(),
        out_shape=pltpu.VMEM(value.shape, value.dtype),
        scratch_shapes=[pltpu.SemaphoreType.DMA((count,))],
        compiler_params=params(),
        cost_estimate=pl.CostEstimate(
            flops=0, transcendentals=0, bytes_accessed=2 * value.size * value.dtype.itemsize
        ),
        name="load",
    )(value)


def load_all_kernel(up, place_ref, *refs):
    *source_refs, out_ref, sem = refs
    count = len(source_refs)
    copies = []
    for k, ref in enumerate(source_refs):
        away = -k if k < up else k - up + 1
        at = lax.rem(place_ref[0] + count + away, count)
        copies.append(pltpu.make_async_copy(ref, out_ref.at[at], sem.at[k]))
        copies[k].start()
    for copy in copies:
        copy.wait()


def load_all(place, values, nz):
    count = len(values)
    shape = (count,) + values[0].shape
    return pl.pallas_call(
        functools.partial(load_all_kernel, count // 2 + 1),
        in_specs=[whole(pltpu.SMEM)] + [whole(pl.ANY)] * count,
        out_specs=whole(),
        out_shape=pltpu.VMEM(shape, values[0].dtype),
        scratch_shapes=[pltpu.SemaphoreType.DMA((count,))],
        compiler_params=params(),
        name="load_all",
    )(place, *values)


def project_kernel(place_ref, *refs):
    *mixed_refs, weight_ref, theirs_ref, ours_ref, rows_ref = refs
    count = len(mixed_refs)
    height = mixed_refs[0].shape[0]
    for k, ref in enumerate(mixed_refs):
        at = lax.rem(place_ref[0] + count - k, count) * height
        rows_ref[pl.ds(pl.multiple_of(at, height), height), :] = ref[...]
    half = ours_ref.shape[0]
    core, odd = place_ref[1], place_ref[2]
    for out_ref, first in ((theirs_ref, (1 - core) * half), (ours_ref, core * half)):
        for i in range(half):
            block = first + lax.rem(i + odd * (half // 2), half)
            out_ref[i] = jnp.dot(
                rows_ref[...], weight_ref[block], preferred_element_type=F32
            ).astype(out_ref.dtype)


def project(place, mixed, weight):
    height, depth = mixed[0].shape
    blocks, _, width = weight.shape
    rows = height * len(mixed)
    shape = (blocks // 2, rows, width)
    return pl.pallas_call(
        project_kernel,
        in_specs=[whole(pltpu.SMEM)] + [whole()] * (len(mixed) + 1),
        out_specs=[whole(), whole()],
        out_shape=[jax.ShapeDtypeStruct(shape, BF16), jax.ShapeDtypeStruct(shape, F32)],
        scratch_shapes=[pltpu.VMEM((rows, depth), BF16)],
        compiler_params=params(),
        name="project",
    )(place, *mixed, weight)


def sum_kernel(*refs):
    *piece_refs, out_ref = refs
    total = sum(ref[...].astype(F32) for ref in piece_refs)
    out_ref[...] = total.reshape(out_ref.shape).astype(BF16)


def sum_pieces(pieces, steps):
    rows, width = pieces[0].shape
    return pl.pallas_call(
        sum_kernel,
        in_specs=[whole()] * len(pieces),
        out_specs=whole(),
        out_shape=jax.ShapeDtypeStruct((rows // steps, steps, width), BF16),
        compiler_params=params(),
        name="sum_pieces",
    )(*pieces)


def per_device(nz, nx, ny, queries, new_kv, prefix_kv, suffix_kv, suffix_len, branch_prompt, out_weight):
    branches, steps, qwidth = queries.shape
    group = qwidth // HEAD_DIM
    height = steps * group
    cache, tensor = lax.axis_index("cache"), lax.axis_index("tensor")
    x, y, core = cache % nx, tensor // 2, tensor % 2
    z_groups = [[z * nx + i for z in range(nz)] for i in range(nx)]

    def along_x(value, k):
        pairs = [(z * nx + i, z * nx + (i + k) % nx) for z in range(nz) for i in range(nx)]
        return lax.ppermute(value, "cache", pairs)

    def along_z(value, k):
        pairs = [(z * nx + i, (z + k) % nz * nx + i) for z in range(nz) for i in range(nx)]
        return lax.ppermute(value, "cache", pairs)

    prompt_ids = branch_prompt[:, 0]
    up, down = [out_weight], [out_weight]

    def pass_on(steps_up, steps_down):
        if steps_up:
            up.append(along_z(up[-1], 1))
        if steps_down:
            down.append(along_z(down[-1], nz - 1))

    def after(value):
        value, up[-1], down[-1] = lax.optimization_barrier((value, up[-1], down[-1]))
        return value

    pass_on(1, 1)
    packed, q_rows = pack(prompt_ids, queries, group)
    mine = lax.all_to_all(packed, "cache", 0, 0, axis_index_groups=z_groups, tiled=True)
    kv = load(prefix_kv, 2)
    mine, kv = lax.optimization_barrier((mine, kv))
    mine = after(mine)
    pass_on(1, 1)
    mine = mine.reshape(nz * SLOTS * height, HEAD_DIM)
    sent = [along_x(mine, k) for k in range(1, nx)]
    fresh = jnp.pad(new_kv.transpose(0, 2, 1, 3), ((0, 0), (0, 0), (0, 16 - steps), (0, 0)))
    own, own_lse = suffix(suffix_len, q_rows, suffix_kv, fresh, steps)
    parts = [attend(mine, kv)]
    for k in range(1, nx):
        part = attend(sent[k - 1], kv)
        if k == 1:
            part = after(part)
            pass_on(1, 1)
        if k == 3:
            part = after(part)
            pass_on(1, 0)
        parts.append(along_x(part, nx - k))
    merged = merge(parts, nz)
    back = lax.all_to_all(merged, "cache", 0, 0, axis_index_groups=z_groups, tiled=True)
    home = (cache // nx).reshape(1)
    mixed = finish(prompt_ids, home, back, own, own_lse, steps, group)
    plane = [mixed] + [along_x(mixed, k) for k in range(1, nx)]
    half = nz // 2
    theirs, ours = project(jnp.stack([x, core, y % 2]), plane, load_all(home, up + down[1:], nz))
    theirs = lax.ppermute(theirs, "tensor", [(t, t ^ 1) for t in range(2 * ny)])
    keep = ours[:2] + theirs[:2].astype(F32)
    give = (ours[2:] + theirs[2:].astype(F32)).astype(BF16)
    keep = (keep + lax.ppermute(give, "tensor", [(t, t ^ 2) for t in range(2 * ny)])).astype(BF16)
    pieces = []
    for k in range(2):
        pairs = [
            (
                ((z * nx + i) * ny + j) * 2 + c,
                ((c * half + (j % 2) * 2 + (k + j // 2) % 2) * nx + i) * 2 * ny + z,
            )
            for z in range(nz)
            for i in range(nx)
            for j in range(ny)
            for c in range(2)
        ]
        block = lax.dynamic_index_in_dim(keep, (k + y // 2) % 2, 0, keepdims=False)
        pieces.append(lax.ppermute(block, ("cache", "tensor"), pairs))
    return sum_pieces(pieces, steps)


def solution(mesh):
    ncache, ntensor = mesh.shape["cache"], mesh.shape["tensor"]
    nz = PROMPTS
    return jax.shard_map(
        functools.partial(per_device, nz, ncache // nz, ntensor // 2),
        mesh=mesh,
        in_specs=(
            P("cache", None, "tensor"),
            P("cache", None, None, "tensor"),
            P(None, "cache", "tensor"),
            P("cache", None, None, "tensor"),
            P("cache"),
            P("cache", None),
            P("tensor", "cache"),
        ),
        out_specs=P("tensor", None, "cache"),
        check_vma=False,
    )
```

```python
import functools

import jax
import jax.numpy as jnp
from jax import lax
from jax.experimental import pallas as pl
from jax.experimental.pallas import tpu as pltpu
from jax.sharding import PartitionSpec as P

HEAD_DIM = 128
PROMPT_LEN = 24576
PROMPTS = 8
SLOTS = 2
LOG2E = 1.4426950408889634
SCORE = LOG2E * HEAD_DIM ** (-0.5)
PART = 512
LARGE = 2.0**100
VMEM_LIMIT = 48 * 1024 * 1024
F32 = jnp.float32
BF16 = jnp.bfloat16


def params():
    return pltpu.CompilerParams(vmem_limit_bytes=VMEM_LIMIT)


def whole(memory_space=pltpu.VMEM):
    return pl.BlockSpec(memory_space=memory_space)


def rank_of(prompt_ref, b):
    rank = jnp.int32(0)
    for earlier in range(b):
        rank += (prompt_ref[earlier] == prompt_ref[b]).astype(jnp.int32)
    return rank


def three_terms(value):
    high = value.astype(BF16).astype(F32)
    rest = value - high
    middle = rest.astype(BF16).astype(F32)
    return high, middle, rest - middle


def pack_kernel(
    branches, steps, group, prompt_hbm, q_hbm, packed_ref, rows_ref, prompt_ref, q_ref, sem
):
    height = steps * group
    copies = [
        pltpu.make_async_copy(prompt_hbm, prompt_ref, sem.at[0]),
        pltpu.make_async_copy(q_hbm, q_ref, sem.at[1]),
    ]
    for copy in copies:
        copy.start()
    packed_ref[...] = jnp.zeros_like(packed_ref)
    for copy in copies:
        copy.wait()
    for b in range(branches):
        own = q_ref[b].astype(F32)
        rows = jnp.concatenate(
            [own[:, h * HEAD_DIM : (h + 1) * HEAD_DIM] for h in range(group)], axis=0
        ).astype(BF16)
        rows_ref[b] = rows
        at = pl.multiple_of(rank_of(prompt_ref, b) * height, height)
        packed_ref[prompt_ref[b], pl.ds(at, height), :] = rows


def pack(prompt_ids, queries, group):
    branches, steps, _ = queries.shape
    height = steps * group
    return pl.pallas_call(
        functools.partial(pack_kernel, branches, steps, group),
        in_specs=[whole(pltpu.HBM), whole(pltpu.HBM)],
        out_specs=[whole(), whole()],
        out_shape=[
            jax.ShapeDtypeStruct((PROMPTS, SLOTS * height, HEAD_DIM), BF16),
            jax.ShapeDtypeStruct((branches, height, HEAD_DIM), BF16),
        ],
        scratch_shapes=[
            pltpu.SMEM((branches,), jnp.int32),
            pltpu.VMEM(queries.shape, BF16),
            pltpu.SemaphoreType.DMA((2,)),
        ],
        compiler_params=params(),
        name="pack_queries",
    )(
        pltpu.with_memory_space_constraint(prompt_ids, pltpu.HBM),
        pltpu.with_memory_space_constraint(queries, pltpu.HBM),
    )


def attend_kernel(part, q_ref, kv_ref, out_ref, qt_ref, top_ref, total_ref, acc_ref):
    rows, length = q_ref.shape[0], kv_ref.shape[1]
    qt_ref[...] = q_ref[...].T

    def scores_of(k):
        return jnp.dot(kv_ref[0, pl.ds(k, part), :], qt_ref[...], preferred_element_type=F32)

    def sums_of(k, weights):
        return lax.dot_general(
            kv_ref[1, pl.ds(k, part), :],
            weights.astype(BF16),
            (((0,), (0,)), ((), ())),
            preferred_element_type=F32,
        )

    following = scores_of(0)
    top = jnp.max(following, axis=0, keepdims=True)
    total = jnp.zeros((8, rows), F32)
    acc = jnp.zeros((HEAD_DIM, rows), F32)
    for k in range(0, length, part):
        scores = following
        if k + part < length:
            following = scores_of(k + part)
        weights = jnp.exp2((scores - top) * SCORE)
        total = total + jnp.sum(weights.reshape(part // 8, 8, rows), axis=0)
        acc = acc + sums_of(k, weights)
    total = jnp.sum(total, axis=0, keepdims=True)
    top_ref[...], total_ref[...], acc_ref[...] = top, total, acc

    @pl.when(jnp.logical_not(jnp.max(total) < LARGE))
    def _():
        top_ref[...] = jnp.full((1, rows), -jnp.inf, F32)
        total_ref[...] = jnp.zeros((1, rows), F32)
        acc_ref[...] = jnp.zeros((HEAD_DIM, rows), F32)

        @pl.loop(0, length // part)
        def _(i):
            k = pl.multiple_of(i * part, part)
            scores = scores_of(k)
            top = top_ref[...]
            new_top = jnp.maximum(top, jnp.max(scores, axis=0, keepdims=True))
            weights = jnp.exp2((scores - new_top) * SCORE)
            fade = jnp.exp2((top - new_top) * SCORE)
            total_ref[...] = total_ref[...] * fade + jnp.sum(weights, axis=0, keepdims=True)
            acc_ref[...] = acc_ref[...] * fade + sums_of(k, weights)
            top_ref[...] = new_top

    total = total_ref[...]
    out_ref[0:HEAD_DIM, :] = (acc_ref[...] / total).astype(BF16)
    terms = three_terms(top_ref[...] * SCORE + jnp.log2(total))
    row = lax.broadcasted_iota(jnp.int32, (16, rows), 0)
    stats = jnp.zeros((16, rows), F32)
    for j in range(3):
        stats = jnp.where(row == j, terms[j], stats)
    out_ref[HEAD_DIM : HEAD_DIM + 16, :] = stats.astype(BF16)


def attend(q, kv):
    rows, length = q.shape[0], kv.shape[1]
    return pl.pallas_call(
        functools.partial(attend_kernel, PART),
        in_specs=[whole(), whole()],
        out_specs=whole(),
        out_shape=jax.ShapeDtypeStruct((HEAD_DIM + 16, rows), BF16),
        scratch_shapes=[
            pltpu.VMEM((HEAD_DIM, rows), BF16),
            pltpu.VMEM((1, rows), F32),
            pltpu.VMEM((1, rows), F32),
            pltpu.VMEM((HEAD_DIM, rows), F32),
        ],
        compiler_params=params(),
        cost_estimate=pl.CostEstimate(
            flops=8 * rows * length * HEAD_DIM,
            transcendentals=rows * length,
            bytes_accessed=4 * length * HEAD_DIM,
        ),
        name="prefix_attention",
    )(q, kv)


def suffix_kernel(steps, len_ref, q_ref, kv_ref, new_ref, out_ref, lse_ref):
    length = len_ref[pl.program_id(0)]
    slots = kv_ref.shape[2]
    keys = jnp.concatenate([kv_ref[0, 0], new_ref[0, 0]], axis=0)
    values = jnp.concatenate([kv_ref[0, 1], new_ref[0, 1]], axis=0)
    scores = lax.dot_general(
        q_ref[0], keys, (((1,), (1,)), ((), ())), preferred_element_type=F32
    )
    place = lax.broadcasted_iota(jnp.int32, scores.shape, 1)
    step = lax.broadcasted_iota(jnp.int32, scores.shape, 0) % steps
    live = (place < length) | ((place >= slots) & (place - slots <= step))
    scores = jnp.where(live, scores, -jnp.inf)
    top = jnp.max(scores, axis=1, keepdims=True)
    weights = jnp.exp2((scores - top) * SCORE)
    total = jnp.sum(weights, axis=1, keepdims=True)
    acc = jnp.dot(weights.astype(BF16), values, preferred_element_type=F32)
    out_ref[0] = acc / total
    lse_ref[0] = jnp.broadcast_to(top * SCORE + jnp.log2(total), acc.shape)


def suffix(lengths, q_rows, suffix_kv, fresh, steps):
    branches, height, _ = q_rows.shape
    block = pl.BlockSpec((1, height, HEAD_DIM), lambda i: (i, 0, 0))
    return pl.pallas_call(
        functools.partial(suffix_kernel, steps),
        grid=(branches,),
        in_specs=[
            whole(pltpu.SMEM),
            block,
            pl.BlockSpec((1,) + suffix_kv.shape[1:], lambda i: (i, 0, 0, 0)),
            pl.BlockSpec((1,) + fresh.shape[1:], lambda i: (i, 0, 0, 0)),
        ],
        out_specs=[block, block],
        out_shape=[jax.ShapeDtypeStruct((branches, height, HEAD_DIM), F32)] * 2,
        compiler_params=params(),
        name="suffix_attention",
    )(lengths, q_rows, suffix_kv, fresh)


def merge_kernel(homes, *refs):
    *part_refs, out_ref = refs
    parts = [ref[...].astype(F32) for ref in part_refs]
    lses = [jnp.sum(p[HEAD_DIM : HEAD_DIM + 3], axis=0, keepdims=True) for p in parts]
    top = functools.reduce(jnp.maximum, lses)
    shares = [jnp.exp2(lse - top) for lse in lses]
    total = sum(shares)
    acc = sum(p[0:HEAD_DIM] * share for p, share in zip(parts, shares, strict=True))
    rows = acc.shape[1]
    height = rows // homes
    out_ref[:, 0:height, :] = (acc / total).T.astype(BF16).reshape(homes, height, HEAD_DIM)
    terms = three_terms(top + jnp.log2(total))
    row = lax.broadcasted_iota(jnp.int32, (16, rows), 0)
    stats = jnp.zeros((16, rows), F32)
    for j in range(3):
        stats = jnp.where(row == j, terms[j], stats)
    stats = stats.astype(BF16)
    for home in range(homes):
        at = home * height // HEAD_DIM * HEAD_DIM
        out_ref[home, height : height + 16, :] = stats[:, at : at + HEAD_DIM]


def merge(parts, homes):
    height = parts[0].shape[1] // homes
    return pl.pallas_call(
        functools.partial(merge_kernel, homes),
        in_specs=[whole()] * len(parts),
        out_specs=whole(),
        out_shape=jax.ShapeDtypeStruct((homes, height + 16, HEAD_DIM), BF16),
        compiler_params=params(),
        name="merge_parts",
    )(*parts)


def finish_kernel(steps, group, prompt_ref, home_ref, back_ref, own_ref, lse_ref, out_ref, col_ref):
    branches, height, _ = own_ref.shape
    tall = SLOTS * height
    lanes = (home_ref[0] * tall) % HEAD_DIM
    pieces = []
    for b in range(branches):
        prompt = prompt_ref[b]
        at = pl.multiple_of(rank_of(prompt_ref, b) * height, height)
        part = back_ref[prompt, pl.ds(at, height), :].astype(F32)
        stats = back_ref[prompt, tall : tall + 16, :].astype(F32)
        part_lse = jnp.sum(stats[0:3], axis=0, keepdims=True)
        col_ref[b] = jnp.broadcast_to(part_lse, (HEAD_DIM, HEAD_DIM)).T
        part_lse = col_ref[b, pl.ds(pl.multiple_of(lanes + at, height), height), :]
        own_lse = lse_ref[b]
        top = jnp.maximum(part_lse, own_lse)
        part_share = jnp.exp2(part_lse - top)
        own_share = jnp.exp2(own_lse - top)
        mixed = (part * part_share + own_ref[b] * own_share) / (part_share + own_share)
        pieces.append(
            jnp.concatenate([mixed[h * steps : (h + 1) * steps] for h in range(group)], axis=1)
        )
    out_ref[...] = jnp.concatenate(pieces, axis=0).astype(BF16)


def finish(prompt_ids, home, back, own, lse, steps, group):
    branches = own.shape[0]
    return pl.pallas_call(
        functools.partial(finish_kernel, steps, group),
        in_specs=[whole(pltpu.SMEM), whole(pltpu.SMEM), whole(), whole(), whole()],
        out_specs=whole(),
        out_shape=jax.ShapeDtypeStruct((branches * steps, group * HEAD_DIM), BF16),
        scratch_shapes=[pltpu.VMEM((branches, HEAD_DIM, HEAD_DIM), F32)],
        compiler_params=params(),
        name="finish_attention",
    )(prompt_ids, home, back, own, lse)


def load_kernel(count, source_ref, out_ref, sem):
    size = source_ref.shape[0] // count
    copies = [
        pltpu.make_async_copy(
            source_ref.at[pl.ds(i * size, size)], out_ref.at[pl.ds(i * size, size)], sem.at[i]
        )
        for i in range(count)
    ]
    for copy in copies:
        copy.start()
    for copy in copies:
        copy.wait()


def load(value, count):
    return pl.pallas_call(
        functools.partial(load_kernel, count),
        in_specs=[whole(pl.ANY)],
        out_specs=whole(),
        out_shape=pltpu.VMEM(value.shape, value.dtype),
        scratch_shapes=[pltpu.SemaphoreType.DMA((count,))],
        compiler_params=params(),
        cost_estimate=pl.CostEstimate(
            flops=0, transcendentals=0, bytes_accessed=2 * value.size * value.dtype.itemsize
        ),
        name="load",
    )(value)


def load_all_kernel(up, place_ref, *refs):
    *source_refs, out_ref, sem = refs
    count = len(source_refs)
    copies = []
    for k, ref in enumerate(source_refs):
        away = -k if k < up else k - up + 1
        at = lax.rem(place_ref[0] + count + away, count)
        copies.append(pltpu.make_async_copy(ref, out_ref.at[at], sem.at[k]))
        copies[k].start()
    for copy in copies:
        copy.wait()


def load_all(place, values, nz):
    count = len(values)
    shape = (count,) + values[0].shape
    return pl.pallas_call(
        functools.partial(load_all_kernel, count // 2 + 1),
        in_specs=[whole(pltpu.SMEM)] + [whole(pl.ANY)] * count,
        out_specs=whole(),
        out_shape=pltpu.VMEM(shape, values[0].dtype),
        scratch_shapes=[pltpu.SemaphoreType.DMA((count,))],
        compiler_params=params(),
        name="load_all",
    )(place, *values)


def project_kernel(place_ref, *refs):
    *mixed_refs, weight_ref, theirs_ref, ours_ref, rows_ref = refs
    count = len(mixed_refs)
    height = mixed_refs[0].shape[0]
    for k, ref in enumerate(mixed_refs):
        at = lax.rem(place_ref[0] + count - k, count) * height
        rows_ref[pl.ds(pl.multiple_of(at, height), height), :] = ref[...]
    half = ours_ref.shape[0]
    core, odd = place_ref[1], place_ref[2]
    for out_ref, first in ((theirs_ref, (1 - core) * half), (ours_ref, core * half)):
        for i in range(half):
            block = first + lax.rem(i + odd * (half // 2), half)
            out_ref[i] = jnp.dot(
                rows_ref[...], weight_ref[block], preferred_element_type=F32
            ).astype(out_ref.dtype)


def project(place, mixed, weight):
    height, depth = mixed[0].shape
    blocks, _, width = weight.shape
    rows = height * len(mixed)
    shape = (blocks // 2, rows, width)
    return pl.pallas_call(
        project_kernel,
        in_specs=[whole(pltpu.SMEM)] + [whole()] * (len(mixed) + 1),
        out_specs=[whole(), whole()],
        out_shape=[jax.ShapeDtypeStruct(shape, BF16), jax.ShapeDtypeStruct(shape, F32)],
        scratch_shapes=[pltpu.VMEM((rows, depth), BF16)],
        compiler_params=params(),
        name="project",
    )(place, *mixed, weight)


def sum_kernel(*refs):
    *piece_refs, out_ref = refs
    total = sum(ref[...].astype(F32) for ref in piece_refs)
    out_ref[...] = total.reshape(out_ref.shape).astype(BF16)


def sum_pieces(pieces, steps):
    rows, width = pieces[0].shape
    return pl.pallas_call(
        sum_kernel,
        in_specs=[whole()] * len(pieces),
        out_specs=whole(),
        out_shape=jax.ShapeDtypeStruct((rows // steps, steps, width), BF16),
        compiler_params=params(),
        name="sum_pieces",
    )(*pieces)


def per_device(nz, nx, ny, queries, new_kv, prefix_kv, suffix_kv, suffix_len, branch_prompt, out_weight):
    branches, steps, qwidth = queries.shape
    group = qwidth // HEAD_DIM
    height = steps * group
    cache, tensor = lax.axis_index("cache"), lax.axis_index("tensor")
    x, y, core = cache % nx, tensor // 2, tensor % 2
    z_groups = [[z * nx + i for z in range(nz)] for i in range(nx)]

    def along_x(value, k):
        pairs = [(z * nx + i, z * nx + (i + k) % nx) for z in range(nz) for i in range(nx)]
        return lax.ppermute(value, "cache", pairs)

    def along_z(value, k):
        pairs = [(z * nx + i, (z + k) % nz * nx + i) for z in range(nz) for i in range(nx)]
        return lax.ppermute(value, "cache", pairs)

    prompt_ids = branch_prompt[:, 0]
    up, down = [out_weight], [out_weight]

    def pass_on(steps_up, steps_down):
        if steps_up:
            up.append(along_z(up[-1], 1))
        if steps_down:
            down.append(along_z(down[-1], nz - 1))

    def after(value):
        value, up[-1], down[-1] = lax.optimization_barrier((value, up[-1], down[-1]))
        return value

    pass_on(1, 1)
    packed, q_rows = pack(prompt_ids, queries, group)
    mine = lax.all_to_all(packed, "cache", 0, 0, axis_index_groups=z_groups, tiled=True)
    kv = load(prefix_kv, 2)
    mine, kv = lax.optimization_barrier((mine, kv))
    mine = after(mine)
    pass_on(1, 1)
    mine = mine.reshape(nz * SLOTS * height, HEAD_DIM)
    sent = [along_x(mine, k) for k in range(1, nx)]
    fresh = jnp.pad(new_kv.transpose(0, 2, 1, 3), ((0, 0), (0, 0), (0, 16 - steps), (0, 0)))
    own, own_lse = suffix(suffix_len, q_rows, suffix_kv, fresh, steps)
    parts = [attend(mine, kv)]
    for k in range(1, nx):
        part = attend(sent[k - 1], kv)
        if k == 2:
            part = after(part)
            pass_on(1, 1)
        parts.append(along_x(part, nx - k))
    parts[0] = after(parts[0])
    pass_on(1, 0)
    merged = merge(parts, nz)
    back = lax.all_to_all(merged, "cache", 0, 0, axis_index_groups=z_groups, tiled=True)
    home = (cache // nx).reshape(1)
    mixed = finish(prompt_ids, home, back, own, own_lse, steps, group)
    plane = [mixed] + [along_x(mixed, k) for k in range(1, nx)]
    half = nz // 2
    theirs, ours = project(jnp.stack([x, core, y % 2]), plane, load_all(home, up + down[1:], nz))
    theirs = lax.ppermute(theirs, "tensor", [(t, t ^ 1) for t in range(2 * ny)])
    keep = ours[:2] + theirs[:2].astype(F32)
    give = (ours[2:] + theirs[2:].astype(F32)).astype(BF16)
    keep = (keep + lax.ppermute(give, "tensor", [(t, t ^ 2) for t in range(2 * ny)])).astype(BF16)
    pieces = []
    for k in range(2):
        pairs = [
            (
                ((z * nx + i) * ny + j) * 2 + c,
                ((c * half + (j % 2) * 2 + (k + j // 2) % 2) * nx + i) * 2 * ny + z,
            )
            for z in range(nz)
            for i in range(nx)
            for j in range(ny)
            for c in range(2)
        ]
        block = lax.dynamic_index_in_dim(keep, (k + y // 2) % 2, 0, keepdims=False)
        pieces.append(lax.ppermute(block, ("cache", "tensor"), pairs))
    return sum_pieces(pieces, steps)


def solution(mesh):
    ncache, ntensor = mesh.shape["cache"], mesh.shape["tensor"]
    nz = PROMPTS
    return jax.shard_map(
        functools.partial(per_device, nz, ncache // nz, ntensor // 2),
        mesh=mesh,
        in_specs=(
            P("cache", None, "tensor"),
            P("cache", None, None, "tensor"),
            P(None, "cache", "tensor"),
            P("cache", None, None, "tensor"),
            P("cache"),
            P("cache", None),
            P("tensor", "cache"),
        ),
        out_specs=P("tensor", None, "cache"),
        check_vma=False,
    )
```

```python
import functools

import jax
import jax.numpy as jnp
from jax import lax
from jax.experimental import pallas as pl
from jax.experimental.pallas import tpu as pltpu
from jax.sharding import PartitionSpec as P

HEAD_DIM = 128
PROMPT_LEN = 24576
PROMPTS = 8
SLOTS = 2
LOG2E = 1.4426950408889634
SCORE = LOG2E * HEAD_DIM ** (-0.5)
PART = 512
LARGE = 2.0**100
VMEM_LIMIT = 48 * 1024 * 1024
F32 = jnp.float32
BF16 = jnp.bfloat16


def params():
    return pltpu.CompilerParams(vmem_limit_bytes=VMEM_LIMIT)


def whole(memory_space=pltpu.VMEM):
    return pl.BlockSpec(memory_space=memory_space)


def rank_of(prompt_ref, b):
    rank = jnp.int32(0)
    for earlier in range(b):
        rank += (prompt_ref[earlier] == prompt_ref[b]).astype(jnp.int32)
    return rank


def three_terms(value):
    high = value.astype(BF16).astype(F32)
    rest = value - high
    middle = rest.astype(BF16).astype(F32)
    return high, middle, rest - middle


def pack_kernel(branches, steps, group, prompt_ref, q_ref, packed_ref, rows_ref):
    height = steps * group
    packed_ref[...] = jnp.zeros_like(packed_ref)
    for b in range(branches):
        own = q_ref[b].astype(F32)
        rows = jnp.concatenate(
            [own[:, h * HEAD_DIM : (h + 1) * HEAD_DIM] for h in range(group)], axis=0
        ).astype(BF16)
        rows_ref[b] = rows
        at = pl.multiple_of(rank_of(prompt_ref, b) * height, height)
        packed_ref[prompt_ref[b], pl.ds(at, height), :] = rows


def pack(prompt_ids, queries, group):
    branches, steps, _ = queries.shape
    height = steps * group
    return pl.pallas_call(
        functools.partial(pack_kernel, branches, steps, group),
        in_specs=[whole(pltpu.SMEM), whole()],
        out_specs=[whole(), whole()],
        out_shape=[
            jax.ShapeDtypeStruct((PROMPTS, SLOTS * height, HEAD_DIM), BF16),
            jax.ShapeDtypeStruct((branches, height, HEAD_DIM), BF16),
        ],
        compiler_params=params(),
        name="pack_queries",
    )(prompt_ids, queries)


def attend_kernel(part, q_ref, kv_ref, out_ref, qt_ref, top_ref, total_ref, acc_ref):
    rows, length = q_ref.shape[0], kv_ref.shape[1]
    qt_ref[...] = q_ref[...].T

    def scores_of(k):
        return jnp.dot(kv_ref[0, pl.ds(k, part), :], qt_ref[...], preferred_element_type=F32)

    def sums_of(k, weights):
        return lax.dot_general(
            kv_ref[1, pl.ds(k, part), :],
            weights.astype(BF16),
            (((0,), (0,)), ((), ())),
            preferred_element_type=F32,
        )

    following = scores_of(0)
    top = jnp.max(following, axis=0, keepdims=True)
    total = jnp.zeros((8, rows), F32)
    acc = jnp.zeros((HEAD_DIM, rows), F32)
    for k in range(0, length, part):
        scores = following
        if k + part < length:
            following = scores_of(k + part)
        weights = jnp.exp2((scores - top) * SCORE)
        total = total + jnp.sum(weights.reshape(part // 8, 8, rows), axis=0)
        acc = acc + sums_of(k, weights)
    total = jnp.sum(total, axis=0, keepdims=True)
    top_ref[...], total_ref[...], acc_ref[...] = top, total, acc

    @pl.when(jnp.logical_not(jnp.max(total) < LARGE))
    def _():
        top_ref[...] = jnp.full((1, rows), -jnp.inf, F32)
        total_ref[...] = jnp.zeros((1, rows), F32)
        acc_ref[...] = jnp.zeros((HEAD_DIM, rows), F32)

        @pl.loop(0, length // part)
        def _(i):
            k = pl.multiple_of(i * part, part)
            scores = scores_of(k)
            top = top_ref[...]
            new_top = jnp.maximum(top, jnp.max(scores, axis=0, keepdims=True))
            weights = jnp.exp2((scores - new_top) * SCORE)
            fade = jnp.exp2((top - new_top) * SCORE)
            total_ref[...] = total_ref[...] * fade + jnp.sum(weights, axis=0, keepdims=True)
            acc_ref[...] = acc_ref[...] * fade + sums_of(k, weights)
            top_ref[...] = new_top

    total = total_ref[...]
    out_ref[0:HEAD_DIM, :] = (acc_ref[...] / total).astype(BF16)
    terms = three_terms(top_ref[...] * SCORE + jnp.log2(total))
    row = lax.broadcasted_iota(jnp.int32, (16, rows), 0)
    stats = jnp.zeros((16, rows), F32)
    for j in range(3):
        stats = jnp.where(row == j, terms[j], stats)
    out_ref[HEAD_DIM : HEAD_DIM + 16, :] = stats.astype(BF16)


def attend(q, kv):
    rows, length = q.shape[0], kv.shape[1]
    return pl.pallas_call(
        functools.partial(attend_kernel, PART),
        in_specs=[whole(), whole()],
        out_specs=whole(),
        out_shape=jax.ShapeDtypeStruct((HEAD_DIM + 16, rows), BF16),
        scratch_shapes=[
            pltpu.VMEM((HEAD_DIM, rows), BF16),
            pltpu.VMEM((1, rows), F32),
            pltpu.VMEM((1, rows), F32),
            pltpu.VMEM((HEAD_DIM, rows), F32),
        ],
        compiler_params=params(),
        cost_estimate=pl.CostEstimate(
            flops=8 * rows * length * HEAD_DIM,
            transcendentals=rows * length,
            bytes_accessed=4 * length * HEAD_DIM,
        ),
        name="prefix_attention",
    )(q, kv)


def suffix_kernel(steps, len_ref, q_ref, kv_ref, new_ref, out_ref, lse_ref):
    length = len_ref[pl.program_id(0)]
    slots = kv_ref.shape[2]
    keys = jnp.concatenate([kv_ref[0, 0], new_ref[0, 0]], axis=0)
    values = jnp.concatenate([kv_ref[0, 1], new_ref[0, 1]], axis=0)
    scores = lax.dot_general(
        q_ref[0], keys, (((1,), (1,)), ((), ())), preferred_element_type=F32
    )
    place = lax.broadcasted_iota(jnp.int32, scores.shape, 1)
    step = lax.broadcasted_iota(jnp.int32, scores.shape, 0) % steps
    live = (place < length) | ((place >= slots) & (place - slots <= step))
    scores = jnp.where(live, scores, -jnp.inf)
    top = jnp.max(scores, axis=1, keepdims=True)
    weights = jnp.exp2((scores - top) * SCORE)
    total = jnp.sum(weights, axis=1, keepdims=True)
    acc = jnp.dot(weights.astype(BF16), values, preferred_element_type=F32)
    out_ref[0] = acc / total
    lse_ref[0] = jnp.broadcast_to(top * SCORE + jnp.log2(total), acc.shape)


def suffix(lengths, q_rows, suffix_kv, fresh, steps):
    branches, height, _ = q_rows.shape
    block = pl.BlockSpec((1, height, HEAD_DIM), lambda i: (i, 0, 0))
    return pl.pallas_call(
        functools.partial(suffix_kernel, steps),
        grid=(branches,),
        in_specs=[
            whole(pltpu.SMEM),
            block,
            pl.BlockSpec((1,) + suffix_kv.shape[1:], lambda i: (i, 0, 0, 0)),
            pl.BlockSpec((1,) + fresh.shape[1:], lambda i: (i, 0, 0, 0)),
        ],
        out_specs=[block, block],
        out_shape=[jax.ShapeDtypeStruct((branches, height, HEAD_DIM), F32)] * 2,
        compiler_params=params(),
        name="suffix_attention",
    )(lengths, q_rows, suffix_kv, fresh)


def merge_kernel(homes, *refs):
    *part_refs, out_ref = refs
    parts = [ref[...].astype(F32) for ref in part_refs]
    lses = [jnp.sum(p[HEAD_DIM : HEAD_DIM + 3], axis=0, keepdims=True) for p in parts]
    top = functools.reduce(jnp.maximum, lses)
    shares = [jnp.exp2(lse - top) for lse in lses]
    total = sum(shares)
    acc = sum(p[0:HEAD_DIM] * share for p, share in zip(parts, shares, strict=True))
    rows = acc.shape[1]
    height = rows // homes
    out_ref[:, 0:height, :] = (acc / total).T.astype(BF16).reshape(homes, height, HEAD_DIM)
    terms = three_terms(top + jnp.log2(total))
    row = lax.broadcasted_iota(jnp.int32, (16, rows), 0)
    stats = jnp.zeros((16, rows), F32)
    for j in range(3):
        stats = jnp.where(row == j, terms[j], stats)
    stats = stats.astype(BF16)
    for home in range(homes):
        at = home * height // HEAD_DIM * HEAD_DIM
        out_ref[home, height : height + 16, :] = stats[:, at : at + HEAD_DIM]


def merge(parts, homes):
    height = parts[0].shape[1] // homes
    return pl.pallas_call(
        functools.partial(merge_kernel, homes),
        in_specs=[whole()] * len(parts),
        out_specs=whole(),
        out_shape=jax.ShapeDtypeStruct((homes, height + 16, HEAD_DIM), BF16),
        compiler_params=params(),
        name="merge_parts",
    )(*parts)


def finish_kernel(steps, group, prompt_ref, home_ref, back_ref, own_ref, lse_ref, out_ref, col_ref):
    branches, height, _ = own_ref.shape
    tall = SLOTS * height
    lanes = (home_ref[0] * tall) % HEAD_DIM
    pieces = []
    for b in range(branches):
        prompt = prompt_ref[b]
        at = pl.multiple_of(rank_of(prompt_ref, b) * height, height)
        part = back_ref[prompt, pl.ds(at, height), :].astype(F32)
        stats = back_ref[prompt, tall : tall + 16, :].astype(F32)
        part_lse = jnp.sum(stats[0:3], axis=0, keepdims=True)
        col_ref[b] = jnp.broadcast_to(part_lse, (HEAD_DIM, HEAD_DIM)).T
        part_lse = col_ref[b, pl.ds(pl.multiple_of(lanes + at, height), height), :]
        own_lse = lse_ref[b]
        top = jnp.maximum(part_lse, own_lse)
        part_share = jnp.exp2(part_lse - top)
        own_share = jnp.exp2(own_lse - top)
        mixed = (part * part_share + own_ref[b] * own_share) / (part_share + own_share)
        pieces.append(
            jnp.concatenate([mixed[h * steps : (h + 1) * steps] for h in range(group)], axis=1)
        )
    out_ref[...] = jnp.concatenate(pieces, axis=0).astype(BF16)


def finish(prompt_ids, home, back, own, lse, steps, group):
    branches = own.shape[0]
    return pl.pallas_call(
        functools.partial(finish_kernel, steps, group),
        in_specs=[whole(pltpu.SMEM), whole(pltpu.SMEM), whole(), whole(), whole()],
        out_specs=whole(),
        out_shape=jax.ShapeDtypeStruct((branches * steps, group * HEAD_DIM), BF16),
        scratch_shapes=[pltpu.VMEM((branches, HEAD_DIM, HEAD_DIM), F32)],
        compiler_params=params(),
        name="finish_attention",
    )(prompt_ids, home, back, own, lse)


def load_kernel(count, source_ref, out_ref, sem):
    size = source_ref.shape[0] // count
    copies = [
        pltpu.make_async_copy(
            source_ref.at[pl.ds(i * size, size)], out_ref.at[pl.ds(i * size, size)], sem.at[i]
        )
        for i in range(count)
    ]
    for copy in copies:
        copy.start()
    for copy in copies:
        copy.wait()


def load(value, count):
    return pl.pallas_call(
        functools.partial(load_kernel, count),
        in_specs=[whole(pl.ANY)],
        out_specs=whole(),
        out_shape=pltpu.VMEM(value.shape, value.dtype),
        scratch_shapes=[pltpu.SemaphoreType.DMA((count,))],
        compiler_params=params(),
        cost_estimate=pl.CostEstimate(
            flops=0, transcendentals=0, bytes_accessed=2 * value.size * value.dtype.itemsize
        ),
        name="load",
    )(value)


def load_all_kernel(up, place_ref, *refs):
    *source_refs, out_ref, sem = refs
    count = len(source_refs)
    copies = []
    for k, ref in enumerate(source_refs):
        away = -k if k < up else k - up + 1
        at = lax.rem(place_ref[0] + count + away, count)
        copies.append(pltpu.make_async_copy(ref, out_ref.at[at], sem.at[k]))
        copies[k].start()
    for copy in copies:
        copy.wait()


def load_all(place, values, nz):
    count = len(values)
    shape = (count,) + values[0].shape
    return pl.pallas_call(
        functools.partial(load_all_kernel, count // 2 + 1),
        in_specs=[whole(pltpu.SMEM)] + [whole(pl.ANY)] * count,
        out_specs=whole(),
        out_shape=pltpu.VMEM(shape, values[0].dtype),
        scratch_shapes=[pltpu.SemaphoreType.DMA((count,))],
        compiler_params=params(),
        name="load_all",
    )(place, *values)


def project_kernel(place_ref, *refs):
    *mixed_refs, weight_ref, theirs_ref, ours_ref, rows_ref = refs
    count = len(mixed_refs)
    height = mixed_refs[0].shape[0]
    for k, ref in enumerate(mixed_refs):
        at = lax.rem(place_ref[0] + count - k, count) * height
        rows_ref[pl.ds(pl.multiple_of(at, height), height), :] = ref[...]
    half = ours_ref.shape[0]
    core, odd = place_ref[1], place_ref[2]
    for out_ref, first in ((theirs_ref, (1 - core) * half), (ours_ref, core * half)):
        for i in range(half):
            block = first + lax.rem(i + odd * (half // 2), half)
            out_ref[i] = jnp.dot(
                rows_ref[...], weight_ref[block], preferred_element_type=F32
            ).astype(out_ref.dtype)


def project(place, mixed, weight):
    height, depth = mixed[0].shape
    blocks, _, width = weight.shape
    rows = height * len(mixed)
    shape = (blocks // 2, rows, width)
    return pl.pallas_call(
        project_kernel,
        in_specs=[whole(pltpu.SMEM)] + [whole()] * (len(mixed) + 1),
        out_specs=[whole(), whole()],
        out_shape=[jax.ShapeDtypeStruct(shape, BF16), jax.ShapeDtypeStruct(shape, F32)],
        scratch_shapes=[pltpu.VMEM((rows, depth), BF16)],
        compiler_params=params(),
        name="project",
    )(place, *mixed, weight)


def sum_kernel(*refs):
    *piece_refs, out_ref = refs
    total = sum(ref[...].astype(F32) for ref in piece_refs)
    out_ref[...] = total.reshape(out_ref.shape).astype(BF16)


def sum_pieces(pieces, steps):
    rows, width = pieces[0].shape
    return pl.pallas_call(
        sum_kernel,
        in_specs=[whole()] * len(pieces),
        out_specs=whole(),
        out_shape=jax.ShapeDtypeStruct((rows // steps, steps, width), BF16),
        compiler_params=params(),
        name="sum_pieces",
    )(*pieces)


def per_device(nz, nx, ny, queries, new_kv, prefix_kv, suffix_kv, suffix_len, branch_prompt, out_weight):
    branches, steps, qwidth = queries.shape
    group = qwidth // HEAD_DIM
    height = steps * group
    cache, tensor = lax.axis_index("cache"), lax.axis_index("tensor")
    x, y, core = cache % nx, tensor // 2, tensor % 2
    z_groups = [[z * nx + i for z in range(nz)] for i in range(nx)]

    def along_x(value, k):
        pairs = [(z * nx + i, z * nx + (i + k) % nx) for z in range(nz) for i in range(nx)]
        return lax.ppermute(value, "cache", pairs)

    def along_z(value, k):
        pairs = [(z * nx + i, (z + k) % nz * nx + i) for z in range(nz) for i in range(nx)]
        return lax.ppermute(value, "cache", pairs)

    prompt_ids = branch_prompt[:, 0]
    up, down = [out_weight], [out_weight]

    def pass_on(steps_up, steps_down):
        if steps_up:
            up.append(along_z(up[-1], 1))
        if steps_down:
            down.append(along_z(down[-1], nz - 1))

    def after(value):
        value, up[-1], down[-1] = lax.optimization_barrier((value, up[-1], down[-1]))
        return value

    pass_on(1, 1)
    packed, q_rows = pack(prompt_ids, queries, group)
    mine = lax.all_to_all(packed, "cache", 0, 0, axis_index_groups=z_groups, tiled=True)
    kv = load(prefix_kv, 2)
    mine, kv = lax.optimization_barrier((mine, kv))
    mine = after(mine)
    pass_on(1, 1)
    mine = mine.reshape(nz * SLOTS * height, HEAD_DIM)
    sent = [along_x(mine, k) for k in range(1, nx)]
    fresh = jnp.pad(new_kv.transpose(0, 2, 1, 3), ((0, 0), (0, 0), (0, 16 - steps), (0, 0)))
    own, own_lse = suffix(suffix_len, q_rows, suffix_kv, fresh, steps)
    parts = [attend(mine, kv)]
    for k in range(1, nx):
        part = attend(sent[k - 1], kv)
        if k == 2:
            part = after(part)
            pass_on(1, 1)
        parts.append(along_x(part, nx - k))
    parts[0] = after(parts[0])
    pass_on(1, 0)
    merged = merge(parts, nz)
    back = lax.all_to_all(merged, "cache", 0, 0, axis_index_groups=z_groups, tiled=True)
    home = (cache // nx).reshape(1)
    mixed = finish(prompt_ids, home, back, own, own_lse, steps, group)
    plane = [mixed] + [along_x(mixed, k) for k in range(1, nx)]
    half = nz // 2
    theirs, ours = project(jnp.stack([x, core, y % 2]), plane, load_all(home, up + down[1:], nz))
    theirs = lax.ppermute(theirs, "tensor", [(t, t ^ 1) for t in range(2 * ny)])
    keep = ours[:2] + theirs[:2].astype(F32)
    give = (ours[2:] + theirs[2:].astype(F32)).astype(BF16)
    keep = (keep + lax.ppermute(give, "tensor", [(t, t ^ 2) for t in range(2 * ny)])).astype(BF16)
    pieces = []
    for k in range(2):
        pairs = [
            (
                ((z * nx + i) * ny + j) * 2 + c,
                ((c * half + (j % 2) * 2 + (k + j // 2) % 2) * nx + i) * 2 * ny + z,
            )
            for z in range(nz)
            for i in range(nx)
            for j in range(ny)
            for c in range(2)
        ]
        block = lax.dynamic_index_in_dim(keep, (k + y // 2) % 2, 0, keepdims=False)
        pieces.append(lax.ppermute(block, ("cache", "tensor"), pairs))
    return sum_pieces(pieces, steps)


def solution(mesh):
    ncache, ntensor = mesh.shape["cache"], mesh.shape["tensor"]
    nz = PROMPTS
    return jax.shard_map(
        functools.partial(per_device, nz, ncache // nz, ntensor // 2),
        mesh=mesh,
        in_specs=(
            P("cache", None, "tensor"),
            P("cache", None, None, "tensor"),
            P(None, "cache", "tensor"),
            P("cache", None, None, "tensor"),
            P("cache"),
            P("cache", None),
            P("tensor", "cache"),
        ),
        out_specs=P("tensor", None, "cache"),
        check_vma=False,
    )
```
